32 devices in a mesh: dom: 4 (over z), blk: 8 (over y, x, core).
Axes of the slice: x: 2, y: 2, z: 4, core: 2. Of those that a mesh axis runs over, the one named last changes fastest.
Arguments:
- features_domain: bfloat16 [24576, 1152], P(('dom', 'blk')), may hold values from -6 to 6
- arrival: int32 [24576], P(('dom', 'blk')), may hold values from 0 to 767, as said below
- positions: float32 [24576, 3], P(('dom', 'blk')), may hold values from 0 to 768, as said below
- species: int32 [24576], P(('dom', 'blk')), may hold values from 0 to 88
- block_count: int32 [384], P(('dom', 'blk')), may hold values from 16 to 64, as said below
- pair_block: int32 [384, 3], P(('dom', 'blk')), may hold values from -1 to 383, as said below
- radial_weights: float32 [8, 7, 128], replicated, may hold values from -0.75 to 0.75
- species_weights: float32 [89, 3, 128], replicated, may hold values from -1 to 1
- mix_weight: bfloat16 [128, 128], replicated, may hold values from -0.5 to 0.5
- self_weight: bfloat16 [128, 128], replicated, may hold values from -0.5 to 0.5
- readout: float32 [128], replicated, may hold values from -0.5 to 0.5
Outputs:
- atom_energy: float32 [24576], P(('dom', 'blk'))
- forces: float32 [24576, 3], P(('dom', 'blk'))
- new_features: bfloat16 [24576, 128], P(('dom', 'blk'))
The draws below stay inside these ranges and needn't reach their ends.
Inputs may be any that keep to these rules, and one draw needn't show every extreme that they name: `arrival`: on each device of dom+blk its 768 entries are a permutation of 0 to 767. `pair_block`: entry [b, 0] is b - 1 or -1, entry [b, 1] is b, entry [b, 2] is b + 1 or -1; the lists are symmetric: [b, 2] is b + 1 exactly when [b + 1, 0] is b. The first block has no predecessor and the last no successor. `block_count`: the live atoms of a block are its first slots. `positions`: atoms of blocks that are not paired lie a distance of 1 or more apart.
All inputs are finite; a program needn't handle non-finite values.
Results may differ from the reference program's by a relative error of at most 0.015.
Values may be sent and summed in bfloat16 or wider, within the bound.
No kernel may reach another device: no remote copies, remote signals or barrier semaphores. Data moves between devices by JAX's collectives and lax.ppermute only.
A program may use at most 64 MiB of HBM per device.

```python
import math
import jax
import jax.numpy as jnp
import numpy as np
from jax import lax

C = 128
NB = 8
SPEC = 89
HARM = 9
BLOCK = 64
ATOM_DEV = 768
NDEV = 32
PIECE = 24
ATOMS = 24576
NBLOCKS = 384


def gap_marks_of(key):
    draw_flags = jax.random.randint(jax.random.fold_in(key, 11), (NBLOCKS,), 0, 4)
    gap_marks = (draw_flags == 0).astype(jnp.int32)
    return gap_marks.at[NBLOCKS - 1].set(1)


def draw_pair_block(key, part):
    gap_marks = gap_marks_of(key)
    blocks = jnp.arange(NBLOCKS, dtype=jnp.int32)
    before = jnp.concatenate([jnp.ones((1,), jnp.int32), gap_marks[:-1]])
    left_pair = jnp.where(before == 0, blocks - 1, -1)
    right_pair = jnp.where(gap_marks == 0, blocks + 1, -1)
    return jnp.stack([left_pair, blocks, right_pair], axis=1).astype(jnp.int32)


def draw_positions(key, part):
    gap_marks = gap_marks_of(key)
    blocks = jnp.arange(NBLOCKS, dtype=jnp.int32)
    anchor = (blocks + jnp.cumsum(gap_marks) - gap_marks).astype(jnp.float32)
    offsets = jax.random.uniform(jax.random.fold_in(key, 12), (NBLOCKS, BLOCK, 3), jnp.float32)
    along_axis = anchor[:, None] + offsets[:, :, 0]
    across = 1.5 * offsets[:, :, 1]
    upward = 1.5 * offsets[:, :, 2]
    return jnp.stack([along_axis, across, upward], axis=2).reshape(NBLOCKS * BLOCK, 3).astype(jnp.float32)


def draw_block_count(key, part):
    counts = jax.random.randint(jax.random.fold_in(key, 13), (NBLOCKS,), 16, BLOCK)
    per_device = NBLOCKS // NDEV
    chosen = jax.random.randint(jax.random.fold_in(key, 14), (NDEV, 1), 0, per_device)
    count_grid = counts.reshape(NDEV, per_device)
    filled = jnp.where(jnp.arange(per_device)[None, :] == chosen, BLOCK, count_grid)
    return filled.reshape(NBLOCKS).astype(jnp.int32)


def draw_arrival(key, part):
    device_keys = jax.random.split(jax.random.fold_in(key, 15), NDEV)

    def shuffled(single):
        return jax.random.permutation(single, ATOM_DEV)
    orders = jax.vmap(shuffled)(device_keys)
    return orders.reshape(NDEV * ATOM_DEV).astype(jnp.int32)


def touch_ends(drawn, own_key, low, top_value):
    place = [jax.random.randint(jax.random.fold_in(own_key, axis), (), 0, length) for axis, length in enumerate(drawn.shape)]
    widest = drawn.shape.index(max(drawn.shape))
    neighbour = place[:widest] + [(place[widest] + 1) % drawn.shape[widest]] + place[widest + 1:]
    return drawn.at[tuple(place)].set(low).at[tuple(neighbour)].set(top_value)


def shard_levels(rng, dims, shards, low, largest):
    gain = 1.0
    for position, blocks in shards:
        steps = jax.random.uniform(jax.random.fold_in(jax.random.fold_in(rng, 6), position), (blocks,), jnp.float32, low / len(shards), largest / len(shards))
        gain = gain * jnp.repeat(jnp.exp(steps), dims[position] // blocks).reshape((-1,) + (1,) * (len(dims) - 1 - position))
    return gain


def scatter_about(own_key, extent, deviation, most, cuts=(), kind=jnp.bfloat16):
    values = jax.random.normal(own_key, extent, jnp.float32) * deviation
    if len(cuts) > 0:
        values = shard_levels(own_key, extent, cuts, -0.22, 0.18) * values
    return jnp.clip(values, min=-most, max=most).astype(kind)


def setup_inputs(seed: int = 0) -> dict:
    splits = jax.random.split(jax.random.key(seed), 12)
    features_domain = scatter_about(splits[0], (ATOMS, HARM * C), 1.0, 6.0, ((0, 32),))
    arrival = draw_arrival(jax.random.fold_in(splits[11], 71), 0)
    positions = draw_positions(jax.random.fold_in(splits[11], 71), 0)
    species = touch_ends(jax.random.randint(splits[3], (ATOMS,), 0, SPEC), jax.random.fold_in(splits[3], 1), 0, SPEC - 1).astype(jnp.int32)
    block_count = draw_block_count(jax.random.fold_in(splits[11], 71), 0)
    pair_block = draw_pair_block(jax.random.fold_in(splits[11], 71), 0)
    radial_weights = scatter_about(splits[6], (NB, 7, C), 64 ** -0.5, 0.75, (), jnp.float32)
    species_weights = jnp.clip(jax.random.uniform(splits[7], (SPEC, 3, C), jnp.float32, -1.0, 1.0), -1.0, 1.0)
    mix_weight = scatter_about(splits[8], (C, C), C ** -0.5, 0.5)
    self_weight = scatter_about(splits[9], (C, C), C ** -0.5, 0.5)
    readout = scatter_about(splits[10], (C,), C ** -0.5, 0.5, (), jnp.float32)
    return {"features_domain": features_domain, "arrival": arrival, "positions": positions, "species": species, "block_count": block_count, "pair_block": pair_block, "radial_weights": radial_weights, "species_weights": species_weights, "mix_weight": mix_weight, "self_weight": self_weight, "readout": readout}


ROOT_THREE = math.sqrt(3.0)
DOT_PATH = np.array([0, 5, 5, 5, 6, 6, 6, 6, 6])
CARRY_PATH = np.array([3, 3, 3, 4, 4, 4, 4, 4])

def harmonics(delta_x, delta_y, delta_z):
    return jnp.stack([jnp.ones_like(delta_x), delta_x, delta_y, delta_z, ROOT_THREE * delta_x * delta_y, ROOT_THREE * delta_y * delta_z, 0.5 * (2.0 * delta_z * delta_z - delta_x * delta_x - delta_y * delta_y), ROOT_THREE * delta_z * delta_x, 0.5 * ROOT_THREE * (delta_x * delta_x - delta_y * delta_y)])

def pair_mask(pair_row, block_rows):
    columns = jnp.arange(3 * block_rows, dtype=jnp.int32)
    listed = (pair_row >= 0).astype(jnp.float32)
    slot_mask = jnp.where(columns < block_rows, listed[0], jnp.where(columns < 2 * block_rows, listed[1], listed[2]))
    targets = jnp.arange(block_rows, dtype=jnp.int32)[:, None] + block_rows
    distinct = (targets != columns[None, :]).astype(jnp.float32)
    return slot_mask[None, :] * distinct

def edge_factors(window_pos, pair_keep, basis_count):
    block_rows = pair_keep.shape[0]
    coords = window_pos.T
    centre = coords[:, block_rows:2 * block_rows]
    delta_x = coords[0][None, :] - centre[0][:, None]
    delta_y = coords[1][None, :] - centre[1][:, None]
    delta_z = coords[2][None, :] - centre[2][:, None]
    spread = delta_x * delta_x + delta_y * delta_y + delta_z * delta_z
    envelope = jnp.maximum(1.0 - spread, 0.0) ** 3 * pair_keep
    orders = jnp.arange(basis_count, dtype=jnp.float32) * math.pi
    radial = envelope[None] * jnp.cos(orders[:, None, None] * spread[None])
    return (radial[:, None] * harmonics(delta_x, delta_y, delta_z)[None]).astype(jnp.bfloat16)

def feature_terms(window_feat, radial_weights):
    values = window_feat.astype(jnp.float32)
    dot_terms = (radial_weights[:, None, DOT_PATH, :] * values[None]).astype(jnp.bfloat16)
    lift_terms = (radial_weights[:, None, 1:3, :] * values[None, :, 0:1, :]).astype(jnp.bfloat16)
    carry_terms = (radial_weights[:, None, CARRY_PATH, :] * values[None, :, 1:, :]).astype(jnp.bfloat16)
    return (dot_terms, lift_terms, carry_terms)

def widen(terms):
    return lax.optimization_barrier(terms).astype(jnp.float32)

def block_messages(edges, dot_terms, lift_terms, carry_terms):
    exact = lax.Precision.HIGHEST
    wide_edges = edges.astype(jnp.float32)
    wide_lift = widen(lift_terms)
    scalar = jnp.einsum('nyij,njyc->ic', wide_edges, widen(dot_terms), precision=exact)
    first_order = jnp.einsum('nmij,njc->mic', wide_edges[:, 1:4], wide_lift[:, :, 0], precision=exact)
    second = jnp.einsum('nmij,njc->mic', wide_edges[:, 4:9], wide_lift[:, :, 1], precision=exact)
    carried = jnp.einsum('nij,njyc->yic', wide_edges[:, 0], widen(carry_terms), precision=exact)
    return jnp.concatenate([scalar[None], first_order + carried[0:3], second + carried[3:8]], axis=0)

def atom_outputs(message_rows, gain_rows, self_part, live_rows, mix_weight, self_weight, readout):
    squares = message_rows * message_rows
    basis_rows = message_rows[0] + gain_rows[:, 0] * squares[0] + gain_rows[:, 1] * lax.optimization_barrier(jnp.sum(squares[1:4], axis=0)) + gain_rows[:, 2] * lax.optimization_barrier(jnp.sum(squares[4:9], axis=0))
    rounded = basis_rows.astype(jnp.bfloat16)
    mixed_rows = jnp.dot(rounded, mix_weight, preferred_element_type=jnp.float32) + jnp.dot(self_part, self_weight, preferred_element_type=jnp.float32)
    energy = live_rows * lax.optimization_barrier(jnp.sum(readout[None, :] * jax.nn.silu(mixed_rows), axis=1))
    return (energy, (mixed_rows * live_rows[:, None]).astype(jnp.bfloat16))

def block_outputs(window_pos, window_feat, pair_row, gain_rows, live_rows, radial_weights, mix_weight, self_weight, readout):
    block_rows = gain_rows.shape[0]
    pair_keep = pair_mask(pair_row, block_rows)
    dot_terms, lift_terms, carry_terms = feature_terms(window_feat, radial_weights)

    def messages_of(positions_window):
        edges = edge_factors(positions_window, pair_keep, radial_weights.shape[0])
        return block_messages(edges, dot_terms, lift_terms, carry_terms)
    messages, pull_edges = jax.vjp(messages_of, window_pos)
    self_rows = window_feat[block_rows:2 * block_rows, 0, :]

    def outputs_of(message_rows):
        return atom_outputs(message_rows, gain_rows, self_rows, live_rows, mix_weight, self_weight, readout)
    energy, pull_atoms, features_out = jax.vjp(outputs_of, messages, has_aux=True)
    grad_messages, = pull_atoms(jnp.ones_like(energy))
    grad_window, = pull_edges(grad_messages)
    return (energy, features_out, grad_window)

def reference(features_domain, arrival, positions, species, block_count, pair_block, radial_weights, species_weights, mix_weight, self_weight, readout):
    slot_index = jnp.arange(ATOMS, dtype=jnp.int32)
    device = slot_index // ATOM_DEV
    source_row = arrival // PIECE * ATOM_DEV + device * PIECE + arrival % PIECE
    live_slots = (slot_index % BLOCK < jnp.repeat(block_count, BLOCK)).astype(jnp.int32)
    relaid = jnp.where(live_slots[:, None] > 0, features_domain[source_row], jnp.zeros((), features_domain.dtype))
    feature_view = jnp.pad(relaid, ((BLOCK, BLOCK), (0, 0))).reshape(ATOMS + 2 * BLOCK, 9, -1)
    position_ext = jnp.pad(positions, ((BLOCK, BLOCK), (0, 0)))
    live_float = live_slots.astype(jnp.float32)

    def scan_step(force_ext, block_index):
        start_row = block_index * BLOCK
        window_pos = lax.dynamic_slice_in_dim(position_ext, start_row, 3 * BLOCK, 0)
        window_feat = lax.dynamic_slice_in_dim(feature_view, start_row, 3 * BLOCK, 0)
        pair_row = lax.dynamic_index_in_dim(pair_block, block_index, 0, keepdims=False)
        species_rows = lax.dynamic_slice_in_dim(species, start_row, BLOCK, 0)
        gain_rows = species_weights[species_rows]
        live_rows = lax.dynamic_slice_in_dim(live_float, start_row, BLOCK, 0)
        energy, features_out, grad_window = block_outputs(window_pos, window_feat, pair_row, gain_rows, live_rows, radial_weights, mix_weight, self_weight, readout)
        current = lax.dynamic_slice_in_dim(force_ext, start_row, 3 * BLOCK, 0)
        force_ext = lax.dynamic_update_slice_in_dim(force_ext, current + grad_window, start_row, 0)
        return (force_ext, (energy, features_out))
    force_ext, (energies, new_rows) = lax.scan(scan_step, jnp.zeros((ATOMS + 2 * BLOCK, 3), jnp.float32), jnp.arange(NBLOCKS, dtype=jnp.int32))
    forces = -force_ext[BLOCK:ATOMS + BLOCK]
    return (energies.reshape(ATOMS), forces, new_rows.reshape(ATOMS, -1))
```

```python
import functools
import math

import jax
import jax.numpy as jnp
import numpy as np
from jax import lax
from jax.experimental import pallas as pl
from jax.experimental.pallas import tpu as pltpu
from jax.sharding import PartitionSpec as P

BLOCK = 64
TILE = 2 * BLOCK
WINDOW = 4 * BLOCK
HARM = 9
ROOT_THREE = math.sqrt(3.0)
AXES = ("dom", "blk")
VMEM_BYTES = 56 * 1024 * 1024


def degree(k):
    return 0 if k == 0 else (1 if k < 4 else 2)


def relay_kernel(arrival_ref, received_ref, relaid_ref):
    rows = received_ref.shape[0]
    wanted = jnp.transpose(jnp.broadcast_to(arrival_ref[...], (8, rows)))[:, 0:1]
    source = lax.broadcasted_iota(jnp.int32, (TILE, rows), 1)
    for part in range(rows // TILE):
        here = slice(part * TILE, (part + 1) * TILE)
        chosen = (wanted[here] == source).astype(jnp.float32).astype(jnp.bfloat16)
        relaid_ref[here, :] = jnp.dot(
            chosen, received_ref[...], preferred_element_type=jnp.float32
        ).astype(jnp.bfloat16)


def relay(arrival_live, received):
    rows, cols = received.shape
    return pl.pallas_call(
        relay_kernel,
        out_shape=jax.ShapeDtypeStruct((rows, cols), jnp.bfloat16),
        in_specs=[pl.BlockSpec(memory_space=pltpu.VMEM)] * 2,
        out_specs=pl.BlockSpec(memory_space=pltpu.VMEM),
        compiler_params=pltpu.CompilerParams(vmem_limit_bytes=VMEM_BYTES),
        cost_estimate=pl.CostEstimate(
            flops=2 * rows * rows * cols, bytes_accessed=4 * rows * cols, transcendentals=0
        ),
        name="relay",
    )(arrival_live, received)


def polynomial(square, coefficients):
    total = jnp.full_like(square, coefficients[-1])
    for value in coefficients[-2::-1]:
        total = total * square + value
    return total


SINE = [(-1.0) ** m * math.pi ** (2 * m + 1) / math.factorial(2 * m + 1) for m in range(6)]
COSINE = [(-1.0) ** m * math.pi ** (2 * m) / math.factorial(2 * m) for m in range(7)]


def solid(x, y, z):
    return [
        None,
        x,
        y,
        z,
        ROOT_THREE * x * y,
        ROOT_THREE * y * z,
        z * z - 0.5 * (x * x + y * y),
        ROOT_THREE * z * x,
        (0.5 * ROOT_THREE) * (x * x - y * y),
    ]


def layer_kernel(
    pair_ref,
    rows_ref,
    relaid_ref,
    low_ref,
    high_ref,
    gains_ref,
    radial_ref,
    mix_ref,
    self_ref,
    readout_ref,
    energy_ref,
    force_ref,
    new_ref,
    feat_ref,
    cols_ref,
    edge_ref,
    radial_val_ref,
    radial_der_ref,
    message_ref,
    grad_ref,
    orders,
):
    step = pl.program_id(0)
    atom_rows = relaid_ref.shape[0]
    channels = mix_ref.shape[0]

    @pl.when(step == 0)
    def _():
        feat_ref[0:BLOCK, :] = low_ref[...]
        feat_ref[BLOCK : BLOCK + atom_rows, :] = relaid_ref[...]
        feat_ref[BLOCK + atom_rows :, :] = high_ref[...]
        cols_ref[...] = jnp.transpose(rows_ref[...])
        force_ref[...] = jnp.zeros_like(force_ref)

    base = pl.multiple_of(step * TILE, TILE)
    window = pl.ds(base, WINDOW)
    centre = pl.ds(pl.multiple_of(base + BLOCK, BLOCK), TILE)

    columns = lax.broadcasted_iota(jnp.int32, (BLOCK, WINDOW), 1)
    targets = lax.broadcasted_iota(jnp.int32, (BLOCK, WINDOW), 0)
    keep_parts = []
    for half in range(2):
        listed = [pair_ref[(2 * step + half) * 3 + side] >= 0 for side in range(3)]
        offset = columns - half * BLOCK
        inside = jnp.zeros((BLOCK, WINDOW), jnp.float32)
        for side in range(3):
            member = (offset >= side * BLOCK) & (offset < (side + 1) * BLOCK)
            inside = jnp.where(member, listed[side].astype(jnp.float32), inside)
        keep_parts.append(jnp.where(targets + BLOCK == offset, 0.0, inside))
    keep = jnp.concatenate(keep_parts, axis=0)

    def deltas():
        return [rows_ref[a : a + 1, window] - cols_ref[centre, a : a + 1] for a in range(3)]

    x, y, z = deltas()
    spread = x * x + y * y + z * z
    room = jnp.maximum(1.0 - spread, 0.0)
    squared = room * room * keep
    envelope = squared * room
    slope = -3.0 * squared
    shifted = jnp.minimum(spread, 1.0) - 0.5
    shifted_sq = shifted * shifted
    cosine = -shifted * polynomial(shifted_sq, SINE)
    sine = polynomial(shifted_sq, COSINE)
    twice = 2.0 * cosine
    cos_prev, cos_now = jnp.ones_like(cosine), cosine
    sin_prev, sin_now = jnp.zeros_like(sine), sine
    harm = solid(x, y, z)
    for n in range(orders):
        here = slice(n * TILE, (n + 1) * TILE)
        if n == 0:
            value, change = envelope, slope
        else:
            value = envelope * cos_now
            change = slope * cos_now - (n * math.pi) * (envelope * sin_now)
        radial_val_ref[here, :] = value
        radial_der_ref[here, :] = change
        for k in range(HARM):
            edge = value if k == 0 else value * harm[k]
            edge_ref[k, here, :] = edge.astype(jnp.bfloat16)
        if n >= 1:
            cos_prev, cos_now = cos_now, twice * cos_now - cos_prev
            sin_prev, sin_now = sin_now, twice * sin_now - sin_prev

    def weight(n, path):
        return radial_ref[n * 7 + path : n * 7 + path + 1, :]

    def piece(k):
        return feat_ref[window, k * channels : (k + 1) * channels]

    def path_sum(product, first, path):
        total = None
        for n in range(orders):
            part = product[n * TILE : (n + 1) * TILE, first : first + channels] * weight(n, path)
            total = part if total is None else total + part
        return total

    scalar = None
    for k in range(HARM):
        pairs = jnp.dot(edge_ref[0], piece(k), preferred_element_type=jnp.float32)
        if k == 0:
            scalar = path_sum(pairs, 0, 0)
        else:
            message_ref[k] = path_sum(pairs, 0, 2 + degree(k))
    message_ref[0] = scalar
    for k in range(1, HARM):
        both = jnp.concatenate([piece(k), piece(0)], axis=1)
        pairs = jnp.dot(edge_ref[k], both, preferred_element_type=jnp.float32)
        message_ref[0] += path_sum(pairs, 0, 4 + degree(k))
        message_ref[k] += path_sum(pairs, channels, degree(k))

    own = pl.ds(base, TILE)
    gain = [gains_ref[own, l * channels : (l + 1) * channels] for l in range(3)]
    zero = message_ref[0]
    first = sum(message_ref[k] * message_ref[k] for k in range(1, 4))
    second = sum(message_ref[k] * message_ref[k] for k in range(4, HARM))
    basis = zero + gain[0] * (zero * zero) + gain[1] * first + gain[2] * second
    live = cols_ref[centre, 3:4]
    mixed = jnp.dot(
        basis.astype(jnp.bfloat16), mix_ref[...], preferred_element_type=jnp.float32
    ) + jnp.dot(feat_ref[centre, 0:channels], self_ref[...], preferred_element_type=jnp.float32)
    gate = 1.0 / (1.0 + jnp.exp(-mixed))
    silu = mixed * gate
    readout = readout_ref[...]
    new_ref[own, :] = (live * mixed).astype(jnp.bfloat16)
    energy_ref[0] = jnp.sum(jnp.transpose(live * (readout * silu)), axis=0, keepdims=True)
    mixed_grad = live * readout * (gate * (1.0 + mixed - silu))
    basis_grad = lax.dot_general(
        mixed_grad.astype(jnp.bfloat16),
        mix_ref[...],
        (((1,), (1,)), ((), ())),
        preferred_element_type=jnp.float32,
    )
    grad_ref[0] = (basis_grad * (1.0 + 2.0 * gain[0] * zero)).astype(jnp.bfloat16)
    for k in range(1, HARM):
        grad_ref[k] = (basis_grad * (2.0 * gain[degree(k)]) * message_ref[k]).astype(jnp.bfloat16)

    def against(left, right):
        return lax.dot_general(
            left, right, (((1,), (1,)), ((), ())), preferred_element_type=jnp.float32
        )

    def narrow(n, path):
        return weight(n, path).astype(jnp.bfloat16)

    x, y, z = deltas()
    left = jnp.concatenate(
        [
            jnp.concatenate(
                [grad_ref[k] * narrow(n, 0 if k == 0 else 2 + degree(k)) for k in range(HARM)],
                axis=1,
            )
            for n in range(orders)
        ],
        axis=0,
    )
    cross = against(left, feat_ref[window, :])
    radial_total = sum(
        cross[n * TILE : (n + 1) * TILE] * radial_der_ref[n * TILE : (n + 1) * TILE, :]
        for n in range(orders)
    )
    root_x, root_y, root_z = ROOT_THREE * x, ROOT_THREE * y, ROOT_THREE * z
    slopes = {
        1: {0: None},
        2: {1: None},
        3: {2: None},
        4: {0: root_y, 1: root_x},
        5: {1: root_z, 2: root_y},
        6: {0: -x, 1: -y, 2: 2.0 * z},
        7: {0: root_z, 2: root_x},
        8: {0: root_x, 1: -root_y},
    }
    pull = [None, None, None]
    harm = solid(x, y, z)
    for k in range(1, HARM):
        left = jnp.concatenate(
            [
                jnp.concatenate(
                    [
                        grad_ref[0] * narrow(n, 4 + degree(k)),
                        grad_ref[k] * narrow(n, degree(k)),
                    ],
                    axis=1,
                )
                for n in range(orders)
            ],
            axis=0,
        )
        cross = against(left, jnp.concatenate([piece(k), piece(0)], axis=1))
        along = None
        turned = None
        for n in range(orders):
            here = slice(n * TILE, (n + 1) * TILE)
            part = cross[here]
            one = part * radial_val_ref[here, :]
            two = part * radial_der_ref[here, :]
            along = one if along is None else along + one
            turned = two if turned is None else turned + two
        radial_total = radial_total + turned * harm[k]
        for axis, factor in slopes[k].items():
            term = along if factor is None else along * factor
            pull[axis] = term if pull[axis] is None else pull[axis] + term
    radial_total = 2.0 * radial_total
    columns_out = []
    for axis, delta in enumerate((x, y, z)):
        total = pull[axis] + delta * radial_total
        force_ref[axis : axis + 1, window] -= jnp.sum(total, axis=0, keepdims=True)
        columns_out.append(jnp.sum(total, axis=1, keepdims=True))
    lane = lax.broadcasted_iota(jnp.int32, (TILE, 8), 1)
    packed = jnp.zeros((TILE, 8), jnp.float32)
    for axis in range(3):
        packed = jnp.where(lane == axis, columns_out[axis], packed)
    turned = jnp.transpose(packed)
    padded = jnp.concatenate(
        [jnp.zeros((8, BLOCK), jnp.float32), turned, jnp.zeros((8, BLOCK), jnp.float32)], axis=1
    )
    force_ref[:, window] += padded


def layer(pair, rows, relaid, low, high, gains, radial, mix, self_weight, readout):
    atom_rows, cols = relaid.shape
    channels = mix.shape[0]
    orders = radial.shape[0] // 7
    wide = atom_rows + 2 * BLOCK
    tiles = atom_rows // TILE
    whole = pl.BlockSpec(memory_space=pltpu.VMEM)
    return pl.pallas_call(
        functools.partial(layer_kernel, orders=orders),
        grid=(tiles,),
        out_shape=(
            jax.ShapeDtypeStruct((tiles, 1, TILE), jnp.float32),
            jax.ShapeDtypeStruct((8, wide), jnp.float32),
            jax.ShapeDtypeStruct((atom_rows, channels), jnp.bfloat16),
        ),
        in_specs=[pl.BlockSpec(memory_space=pltpu.SMEM)] + [whole] * 9,
        out_specs=(
            pl.BlockSpec((1, 1, TILE), lambda t: (t, 0, 0)),
            whole,
            whole,
        ),
        scratch_shapes=[
            pltpu.VMEM((wide, cols), jnp.bfloat16),
            pltpu.VMEM((wide, 8), jnp.float32),
            pltpu.VMEM((HARM, orders * TILE, WINDOW), jnp.bfloat16),
            pltpu.VMEM((orders * TILE, WINDOW), jnp.float32),
            pltpu.VMEM((orders * TILE, WINDOW), jnp.float32),
            pltpu.VMEM((HARM, TILE, channels), jnp.float32),
            pltpu.VMEM((HARM, TILE, channels), jnp.bfloat16),
        ],
        compiler_params=pltpu.CompilerParams(vmem_limit_bytes=VMEM_BYTES),
        cost_estimate=pl.CostEstimate(
            flops=tiles * 4 * orders * TILE * WINDOW * channels * 25,
            bytes_accessed=4 * atom_rows * cols,
            transcendentals=0,
        ),
        name="layer",
    )(pair, rows, relaid, low, high, gains, radial, mix, self_weight, readout)


def from_sides(block_low, block_high):
    count = lax.axis_size(AXES)
    forward = [(i, i + 1) for i in range(count - 1)]
    backward = [(target, source) for source, target in forward]
    low = lax.ppermute(block_high, AXES, forward)
    high = lax.ppermute(block_low, AXES, backward)
    return low, high


def per_device(
    features_domain,
    arrival,
    positions,
    species,
    block_count,
    pair_block,
    radial_weights,
    species_weights,
    mix_weight,
    self_weight,
    readout,
):
    devices = lax.axis_size(AXES)
    atom_rows, feature_cols = features_domain.shape
    piece_rows = atom_rows // devices
    parcels = features_domain.reshape(devices, piece_rows, feature_cols)
    received = lax.all_to_all(parcels, AXES, split_axis=0, concat_axis=0, tiled=True)
    received = received.reshape(atom_rows, feature_cols)
    slot_index = jnp.arange(atom_rows, dtype=jnp.int32)
    live = slot_index % BLOCK < jnp.repeat(block_count, BLOCK, total_repeat_length=atom_rows)
    arrival_live = jnp.where(live, arrival, -1).reshape(1, atom_rows)
    coords = positions.T
    low_pos, high_pos = from_sides(coords[:, :BLOCK], coords[:, atom_rows - BLOCK :])
    coords = jnp.concatenate([low_pos, coords, high_pos], axis=1)
    live_row = jnp.pad(live.astype(jnp.float32), (BLOCK, BLOCK)).reshape(1, -1)
    rows = jnp.concatenate([coords, live_row, jnp.zeros((4, coords.shape[1]), jnp.float32)], axis=0)
    species_total = species_weights.shape[0]
    one_hot = (species[:, None] == jnp.arange(species_total, dtype=jnp.int32)[None, :]).astype(
        jnp.float32
    )
    gains = jnp.dot(
        one_hot, species_weights.reshape(species_total, -1), precision=lax.Precision.HIGHEST
    )
    relaid = relay(arrival_live, received)
    low, high = from_sides(relaid[:BLOCK], relaid[atom_rows - BLOCK :])
    energies, force_ext, new_rows = layer(
        pair_block.reshape(-1),
        rows,
        relaid,
        low,
        high,
        gains,
        radial_weights.reshape(-1, radial_weights.shape[2]),
        mix_weight,
        self_weight,
        readout.reshape(1, -1),
    )
    from_low, from_high = from_sides(force_ext[:3, :BLOCK], force_ext[:3, atom_rows + BLOCK :])
    forces = force_ext[:3, BLOCK : atom_rows + BLOCK]
    forces = forces + jnp.pad(from_low, ((0, 0), (0, atom_rows - BLOCK)))
    forces = forces + jnp.pad(from_high, ((0, 0), (atom_rows - BLOCK, 0)))
    return (energies.reshape(atom_rows), forces.T, new_rows)


def solution(mesh):
    placed = (
        P(("dom", "blk"), None),
        P(("dom", "blk")),
        P(("dom", "blk"), None),
        P(("dom", "blk")),
        P(("dom", "blk")),
        P(("dom", "blk"), None),
        P(),
        P(),
        P(),
        P(),
        P(),
    )
    return jax.shard_map(
        per_device,
        mesh=mesh,
        in_specs=placed,
        out_specs=(P(("dom", "blk")), P(("dom", "blk"), None), P(("dom", "blk"), None)),
        check_vma=False,
    )
```

```python
import functools
import math

import jax
import jax.numpy as jnp
import numpy as np
from jax import lax
from jax.experimental import pallas as pl
from jax.experimental.pallas import tpu as pltpu
from jax.sharding import PartitionSpec as P

BLOCK = 64
TILE = 2 * BLOCK
WINDOW = 4 * BLOCK
SUB = 32
HARM = 9
PATHS = 7
ROOT_THREE = math.sqrt(3.0)
AXES = ("dom", "blk")
VMEM_BYTES = 48 * 1024 * 1024
HELD = pltpu.VMEM


def degree(k):
    return 0 if k == 0 else (1 if k < 4 else 2)


def polynomial(square, coefficients):
    total = jnp.full_like(square, coefficients[-1])
    for value in coefficients[-2::-1]:
        total = total * square + value
    return total


SINE = [(-1.0) ** m * math.pi ** (2 * m + 1) / math.factorial(2 * m + 1) for m in range(6)]
COSINE = [(-1.0) ** m * math.pi ** (2 * m) / math.factorial(2 * m) for m in range(7)]


def solid(x, y, z):
    return [
        None,
        x,
        y,
        z,
        ROOT_THREE * x * y,
        ROOT_THREE * y * z,
        z * z - 0.5 * (x * x + y * y),
        ROOT_THREE * z * x,
        (0.5 * ROOT_THREE) * (x * x - y * y),
    ]


def chosen_rows(wanted, rows):
    source = lax.broadcasted_iota(jnp.int32, (wanted.shape[0], rows), 1)
    return (wanted == source).astype(jnp.float32).astype(jnp.bfloat16)


def as_column(row_ref):
    return jnp.transpose(jnp.broadcast_to(row_ref[...], (8, row_ref.shape[1])))[:, 0:1]


def edge_tiles_kernel(arrival_ref, received_ref, first_ref, last_ref):
    rows = received_ref.shape[0]
    wanted = as_column(arrival_ref)
    both = jnp.concatenate([wanted[0:TILE], wanted[rows - TILE :]], axis=0)
    found = jnp.dot(
        chosen_rows(both, rows), received_ref[...], preferred_element_type=jnp.float32
    ).astype(jnp.bfloat16)
    first_ref[...] = found[0:TILE]
    last_ref[...] = found[TILE:]


def pair_factors(base, rows_ref, cols_ref, edge_at, value_at, change_at, orders):
    window = pl.ds(base, WINDOW)
    for sub in range(TILE // SUB):
        half = sub * SUB // BLOCK
        here = pl.ds(pl.multiple_of(base + (BLOCK + sub * SUB), SUB), SUB)
        column = lax.broadcasted_iota(jnp.int32, (SUB, WINDOW), 1)
        row = lax.broadcasted_iota(jnp.int32, (SUB, WINDOW), 0) + (sub * SUB + BLOCK)
        offset = column - half * BLOCK
        low = jnp.where((offset >= 0) & (offset < BLOCK), cols_ref[here, 5:6], 0.0)
        high = jnp.where(
            (offset >= 2 * BLOCK) & (offset < 3 * BLOCK), cols_ref[here, 6:7], low
        )
        same = (offset >= BLOCK) & (offset < 2 * BLOCK) & (row != column)
        keep = jnp.where(same, 1.0, high)
        x, y, z = [rows_ref[a : a + 1, window] - cols_ref[here, a : a + 1] for a in range(3)]
        spread = x * x + y * y + z * z
        room = jnp.maximum(1.0 - spread, 0.0)
        squared = room * room * keep
        envelope = squared * room
        slope = -3.0 * squared
        shifted = jnp.minimum(spread, 1.0) - 0.5
        shifted_sq = shifted * shifted
        cosine = -shifted * polynomial(shifted_sq, SINE)
        sine = polynomial(shifted_sq, COSINE)
        twice = 2.0 * cosine
        cos_prev, cos_now = jnp.ones_like(cosine), cosine
        sin_prev, sin_now = jnp.zeros_like(sine), sine
        harm = solid(x, y, z)
        for n in range(orders):
            rows = slice(n * SUB, (n + 1) * SUB)
            if n == 0:
                value, change = envelope, slope
            else:
                value = envelope * cos_now
                change = slope * cos_now - (n * math.pi) * (envelope * sin_now)
            value_at[sub, rows, :] = value
            change_at[sub, rows, :] = change
            for k in range(HARM):
                edge = value if k == 0 else value * harm[k]
                edge_at[sub, k, rows, :] = edge.astype(jnp.bfloat16)
            if n >= 1:
                cos_prev, cos_now = cos_now, twice * cos_now - cos_prev
                sin_prev, sin_now = sin_now, twice * sin_now - sin_prev


def pairs_kernel(rows_ref, edge_ref, value_ref, change_ref, cols_ref, orders):
    tile = pl.program_id(0)

    @pl.when(tile == 0)
    def _():
        cols_ref[...] = jnp.transpose(rows_ref[...])

    base = pl.multiple_of(tile * TILE, TILE)
    pair_factors(
        base, rows_ref, cols_ref, edge_ref.at[0], value_ref.at[0], change_ref.at[0], orders
    )


def spread_weights(radial_ref, narrow_ref, orders):
    for path in range(PATHS):
        for n in range(orders):
            row = radial_ref[n * PATHS + path : n * PATHS + path + 1, :]
            narrow_ref[path, n * SUB : (n + 1) * SUB, :] = jnp.broadcast_to(
                row, (SUB, row.shape[1])
            ).astype(jnp.bfloat16)


def fetch(sources, held):
    edge_hbm, value_hbm, change_hbm = sources
    edge_ref, value_ref, change_ref, edge_sem, factor_sem = held
    count, subs = edge_ref.shape[:2]

    def edges(at, sub):
        return pltpu.make_async_copy(
            edge_hbm.at[at, sub], edge_ref.at[at, sub], edge_sem.at[at, sub]
        )

    def factors(at):
        return (
            pltpu.make_async_copy(value_hbm.at[at], value_ref.at[at], factor_sem.at[at, 0]),
            pltpu.make_async_copy(change_hbm.at[at], change_ref.at[at], factor_sem.at[at, 1]),
        )

    for at in range(count):
        for sub in range(subs):
            edges(at, sub).start()
        for copy in factors(at):
            copy.start()
    return edges, factors


def one_tile(at, base, refs, gain_of, copies, results, orders):
    feat_ref, turned_ref, rows_ref, cols_ref, edge_ref, value_ref, change_ref = refs[:7]
    radial_ref, narrow_ref, mix_ref, self_ref, readout_ref = refs[7:12]
    message_ref, grad_ref = refs[12:]
    channels = mix_ref.shape[0]
    window = pl.ds(base, WINDOW)
    centre = pl.ds(pl.multiple_of(base + BLOCK, BLOCK), TILE)
    subs = range(TILE // SUB)

    def weight(n, path):
        return radial_ref[n * PATHS + path : n * PATHS + path + 1, :]

    def piece(k):
        return feat_ref[window, k * channels : (k + 1) * channels]

    def path_sum(product, first, path):
        total = None
        for n in range(orders):
            part = product[n * SUB : (n + 1) * SUB, first : first + channels] * weight(n, path)
            total = part if total is None else total + part
        return total

    for sub in subs:
        rows = slice(sub * SUB, (sub + 1) * SUB)
        if copies is not None:
            copies[0](at, sub).wait()
        for k in range(0, HARM, 2):
            last = min(k + 2, HARM)
            pairs = jnp.dot(
                edge_ref[at, sub, 0],
                feat_ref[window, k * channels : last * channels],
                preferred_element_type=jnp.float32,
            )
            for which in range(k, last):
                path = 0 if which == 0 else 2 + degree(which)
                message_ref[which, rows, :] = path_sum(pairs, (which - k) * channels, path)
        for k in range(1, HARM):
            both = jnp.concatenate([piece(k), piece(0)], axis=1)
            pairs = jnp.dot(edge_ref[at, sub, k], both, preferred_element_type=jnp.float32)
            message_ref[0, rows, :] += path_sum(pairs, 0, 4 + degree(k))
            message_ref[k, rows, :] += path_sum(pairs, channels, degree(k))

    gain = gain_of(centre)
    zero = message_ref[0]
    first = sum(message_ref[k] * message_ref[k] for k in range(1, 4))
    second = sum(message_ref[k] * message_ref[k] for k in range(4, HARM))
    basis = zero + gain[0] * (zero * zero) + gain[1] * first + gain[2] * second
    live = cols_ref[centre, 3:4]
    mixed = jnp.dot(
        basis.astype(jnp.bfloat16), mix_ref[...], preferred_element_type=jnp.float32
    ) + jnp.dot(feat_ref[centre, 0:channels], self_ref[...], preferred_element_type=jnp.float32)
    gate = 1.0 / (1.0 + jnp.exp(-mixed))
    silu = mixed * gate
    readout = readout_ref[...]
    fresh = (live * mixed).astype(jnp.bfloat16)
    energy = jnp.sum(jnp.transpose(live * (readout * silu)), axis=0, keepdims=True)
    mixed_grad = live * readout * (gate * (1.0 + mixed - silu))
    basis_grad = lax.dot_general(
        mixed_grad.astype(jnp.bfloat16),
        mix_ref[...],
        (((1,), (1,)), ((), ())),
        preferred_element_type=jnp.float32,
    )
    grad_ref[0] = (basis_grad * (1.0 + 2.0 * gain[0] * zero)).astype(jnp.bfloat16)
    for k in range(1, HARM):
        grad_ref[k] = (basis_grad * (2.0 * gain[degree(k)]) * message_ref[k]).astype(jnp.bfloat16)

    def backward(sub):
        rows = slice(sub * SUB, (sub + 1) * SUB)
        here = pl.ds(pl.multiple_of(base + (BLOCK + sub * SUB), SUB), SUB)
        grads = [jnp.concatenate([grad_ref[k, rows, :]] * orders, axis=0) for k in range(HARM)]
        x, y, z = [rows_ref[a : a + 1, window] - cols_ref[here, a : a + 1] for a in range(3)]
        harm = solid(x, y, z)
        root_x, root_y, root_z = ROOT_THREE * x, ROOT_THREE * y, ROOT_THREE * z
        slopes = {
            1: {0: None},
            2: {1: None},
            3: {2: None},
            4: {0: root_y, 1: root_x},
            5: {1: root_z, 2: root_y},
            6: {0: -x, 1: -y, 2: 2.0 * z},
            7: {0: root_z, 2: root_x},
            8: {0: root_x, 1: -root_y},
        }

        def over_orders(cross, factor_ref):
            total = None
            for n in range(orders):
                part = cross[n * SUB : (n + 1) * SUB] * factor_ref[
                    at, sub, n * SUB : (n + 1) * SUB, :
                ]
                total = part if total is None else total + part
            return total

        left = jnp.concatenate(
            [grads[k] * narrow_ref[0 if k == 0 else 2 + degree(k)] for k in range(HARM)], axis=1
        )
        cross = jnp.dot(left, turned_ref[:, window], preferred_element_type=jnp.float32)
        radial_total = over_orders(cross, change_ref)
        pull = [None, None, None]
        for k in range(1, HARM):
            left = jnp.concatenate(
                [grads[0] * narrow_ref[4 + degree(k)], grads[k] * narrow_ref[degree(k)]], axis=1
            )
            both = jnp.concatenate(
                [
                    turned_ref[k * channels : (k + 1) * channels, window],
                    turned_ref[0:channels, window],
                ],
                axis=0,
            )
            cross = jnp.dot(left, both, preferred_element_type=jnp.float32)
            along = over_orders(cross, value_ref)
            radial_total = radial_total + over_orders(cross, change_ref) * harm[k]
            for axis, factor in slopes[k].items():
                term = along if factor is None else along * factor
                pull[axis] = term if pull[axis] is None else pull[axis] + term
        radial_total = 2.0 * radial_total
        return [pull[axis] + delta * radial_total for axis, delta in enumerate((x, y, z))]

    if copies is not None:
        for copy in copies[1](at):
            copy.wait()
    onto_window = [None, None, None]
    columns_out = [[], [], []]
    for sub in subs:
        for axis, total in enumerate(backward(sub)):
            summed = jnp.sum(total, axis=0, keepdims=True)
            onto_window[axis] = summed if sub == 0 else onto_window[axis] + summed
            columns_out[axis].append(jnp.sum(total, axis=1, keepdims=True))
    lane = lax.broadcasted_iota(jnp.int32, (TILE, 8), 1)
    row = lax.broadcasted_iota(jnp.int32, (8, WINDOW), 0)
    packed = jnp.zeros((TILE, 8), jnp.float32)
    pulled = jnp.zeros((8, WINDOW), jnp.float32)
    for axis in range(3):
        packed = jnp.where(lane == axis, jnp.concatenate(columns_out[axis], axis=0), packed)
        pulled = jnp.where(row == axis, onto_window[axis], pulled)
    turned = jnp.transpose(packed)
    side = jnp.zeros((8, BLOCK), jnp.float32)
    results(fresh, energy, jnp.concatenate([side, turned, side], axis=1) - pulled)


def inner_kernel(
    arrival_ref,
    received_ref,
    rows_ref,
    edge_hbm,
    value_hbm,
    change_hbm,
    gains_ref,
    radial_ref,
    mix_ref,
    self_ref,
    readout_ref,
    feat_ref,
    new_ref,
    energy_ref,
    force_ref,
    turned_ref,
    cols_ref,
    narrow_ref,
    message_ref,
    grad_ref,
    edge_ref,
    value_ref,
    change_ref,
    edge_sem,
    factor_sem,
    orders,
):
    held = (edge_ref, value_ref, change_ref, edge_sem, factor_sem)
    copies = fetch((edge_hbm, value_hbm, change_hbm), held)
    rows = received_ref.shape[0]
    channels = mix_ref.shape[0]
    wanted = as_column(arrival_ref)
    cols_ref[...] = jnp.transpose(rows_ref[...])
    spread_weights(radial_ref, narrow_ref, orders)
    force_ref[...] = jnp.zeros_like(force_ref)
    for part in range(rows // TILE):
        here = slice(part * TILE, (part + 1) * TILE)
        found = jnp.dot(
            chosen_rows(wanted[here], rows),
            received_ref[...],
            preferred_element_type=jnp.float32,
        ).astype(jnp.bfloat16)
        feat_ref[here, :] = found
        turned_ref[:, here] = jnp.transpose(found)
    refs = (feat_ref, turned_ref, rows_ref, cols_ref, edge_ref, value_ref, change_ref)
    refs += (radial_ref, narrow_ref, mix_ref, self_ref, readout_ref, message_ref, grad_ref)

    def gain_of(centre):
        return [gains_ref[centre, l * channels : (l + 1) * channels] for l in range(3)]

    def body(at, carry):
        base = pl.multiple_of(at * TILE, TILE)

        def results(fresh, energy, force):
            new_ref[at] = fresh
            energy_ref[at] = energy
            force_ref[:, pl.ds(base, WINDOW)] += force

        one_tile(at, base, refs, gain_of, copies, results, orders)
        return carry

    lax.fori_loop(0, edge_hbm.shape[0], body, 0)


def outer_kernel(
    low_ref,
    high_ref,
    feat_ref,
    low_rows_ref,
    rows_ref,
    high_rows_ref,
    table_ref,
    radial_ref,
    mix_ref,
    self_ref,
    readout_ref,
    inner_new_ref,
    inner_energy_ref,
    inner_force_ref,
    new_ref,
    energy_ref,
    force_ref,
    near_ref,
    turned_ref,
    near_rows_ref,
    cols_ref,
    narrow_ref,
    message_ref,
    grad_ref,
    edge_ref,
    value_ref,
    change_ref,
    total_ref,
    orders,
):
    rows = feat_ref.shape[0]
    channels = mix_ref.shape[0]
    near_rows_ref[:, 0:TILE] = low_rows_ref[...]
    near_rows_ref[:, TILE : 2 * TILE] = rows_ref[:, 0:TILE]
    near_rows_ref[:, 2 * TILE : 3 * TILE] = rows_ref[:, rows - TILE :]
    near_rows_ref[:, 3 * TILE :] = high_rows_ref[...]
    cols_ref[...] = jnp.transpose(near_rows_ref[...])
    spread_weights(radial_ref, narrow_ref, orders)
    near_ref[0:TILE, :] = low_ref[...]
    near_ref[TILE : 2 * TILE, :] = feat_ref[0:TILE, :]
    near_ref[2 * TILE : 3 * TILE, :] = feat_ref[rows - TILE :, :]
    near_ref[3 * TILE :, :] = high_ref[...]
    for part in range(4):
        here = slice(part * TILE, (part + 1) * TILE)
        turned_ref[:, here] = jnp.transpose(near_ref[here, :])
    refs = (near_ref, turned_ref, near_rows_ref, cols_ref, edge_ref, value_ref, change_ref)
    refs += (radial_ref, narrow_ref, mix_ref, self_ref, readout_ref, message_ref, grad_ref)

    def gain_of(centre):
        kinds = lax.broadcasted_iota(jnp.int32, (TILE, table_ref.shape[0]), 1)
        picked = (cols_ref[centre, 4:5].astype(jnp.int32) == kinds).astype(jnp.float32)
        rows_of = jnp.dot(
            picked,
            table_ref[...],
            precision=lax.Precision.HIGHEST,
            preferred_element_type=jnp.float32,
        )
        return [rows_of[:, l * channels : (l + 1) * channels] for l in range(3)]

    def body(at, carry):
        base = pl.multiple_of(at * WINDOW, WINDOW)

        def results(fresh, energy, force):
            total_ref[at] = force

            @pl.when(at == 0)
            def _():
                new_ref[0:BLOCK, :] = fresh[BLOCK:, :]
                energy_ref[:, 0:BLOCK] = energy[:, BLOCK:]

            @pl.when(at == 1)
            def _():
                new_ref[rows - BLOCK :, :] = fresh[0:BLOCK, :]
                energy_ref[:, rows - BLOCK :] = energy[:, 0:BLOCK]

        pair_factors(
            base, near_rows_ref, cols_ref, edge_ref.at[at], value_ref.at[at], change_ref.at[at], orders
        )
        one_tile(at, base, refs, gain_of, None, results, orders)
        return carry

    lax.fori_loop(0, 2, body, 0)
    inner = inner_new_ref.shape[0]
    for at in range(inner):
        here = slice(BLOCK + at * TILE, BLOCK + (at + 1) * TILE)
        new_ref[here, :] = inner_new_ref[at]
        energy_ref[:, here] = inner_energy_ref[at]
    force_ref[...] = inner_force_ref[...]
    force_ref[:, 0:TILE] += total_ref[0, :, TILE:]
    force_ref[:, rows - TILE :] += total_ref[1, :, 0:TILE]


def call(kernel, name, out_shape, scratch, flops, *operands, distant=()):
    whole = pl.BlockSpec(memory_space=pltpu.VMEM)
    hbm = pl.BlockSpec(memory_space=pl.ANY)
    return pl.pallas_call(
        kernel,
        out_shape=out_shape,
        in_specs=[hbm if at in distant else whole for at in range(len(operands))],
        out_specs=jax.tree.map(lambda _: whole, out_shape),
        scratch_shapes=scratch,
        compiler_params=pltpu.CompilerParams(vmem_limit_bytes=VMEM_BYTES),
        cost_estimate=pl.CostEstimate(flops=flops, bytes_accessed=4 * 2**20, transcendentals=0),
        name=name,
    )(*operands)


def from_sides(block_low, block_high):
    count = lax.axis_size(AXES)
    forward = [(i, i + 1) for i in range(count - 1)]
    backward = [(target, source) for source, target in forward]
    low = lax.ppermute(block_high, AXES, forward)
    high = lax.ppermute(block_low, AXES, backward)
    return low, high


def per_device(
    features_domain,
    arrival,
    positions,
    species,
    block_count,
    pair_block,
    radial_weights,
    species_weights,
    mix_weight,
    self_weight,
    readout,
):
    devices = lax.axis_size(AXES)
    atom_rows, feature_cols = features_domain.shape
    piece_rows = atom_rows // devices
    parcels = features_domain.reshape(devices, piece_rows, feature_cols)
    received = lax.all_to_all(parcels, AXES, split_axis=0, concat_axis=0, tiled=True)
    received = received.reshape(atom_rows, feature_cols)
    blocks = block_count.shape[0]
    bf16, f32 = jnp.bfloat16, jnp.float32
    shape = jax.ShapeDtypeStruct

    def per_slot(values):
        return jnp.broadcast_to(values[:, None], (blocks, BLOCK)).reshape(1, atom_rows)

    slot = jnp.arange(BLOCK, dtype=jnp.int32)
    live = (slot[None, :] < block_count[:, None]).reshape(1, atom_rows)
    arrival_live = jnp.where(live, arrival.reshape(1, atom_rows), -1)
    listed = (pair_block >= 0).astype(f32)
    rows = jnp.concatenate(
        [
            positions.T,
            live.astype(f32),
            species.astype(f32).reshape(1, atom_rows),
            per_slot(listed[:, 0]),
            per_slot(listed[:, 2]),
            jnp.zeros((1, atom_rows), f32),
        ],
        axis=0,
    )
    low_rows, high_rows = from_sides(rows[:, :TILE], rows[:, atom_rows - TILE :])
    species_total = species_weights.shape[0]
    one_hot = (species[:, None] == jnp.arange(species_total, dtype=jnp.int32)[None, :]).astype(f32)
    table = species_weights.reshape(species_total, -1)
    gains = jnp.dot(one_hot, table, precision=lax.Precision.HIGHEST)
    orders, _, channels = radial_weights.shape
    inner = atom_rows // TILE - 1
    subs = TILE // SUB
    stack = orders * SUB
    edges, values, changes = pl.pallas_call(
        functools.partial(pairs_kernel, orders=orders),
        grid=(inner,),
        out_shape=(
            pltpu.HBM((inner, subs, HARM, stack, WINDOW), bf16),
            pltpu.HBM((inner, subs, stack, WINDOW), f32),
            pltpu.HBM((inner, subs, stack, WINDOW), f32),
        ),
        in_specs=[pl.BlockSpec((8, atom_rows), lambda t: (0, 0))],
        out_specs=(
            pl.BlockSpec((1, subs, HARM, stack, WINDOW), lambda t: (t, 0, 0, 0, 0)),
            pl.BlockSpec((1, subs, stack, WINDOW), lambda t: (t, 0, 0, 0)),
            pl.BlockSpec((1, subs, stack, WINDOW), lambda t: (t, 0, 0, 0)),
        ),
        scratch_shapes=[pltpu.VMEM((atom_rows, 8), f32)],
        compiler_params=pltpu.CompilerParams(vmem_limit_bytes=VMEM_BYTES),
        cost_estimate=pl.CostEstimate(flops=10**10, bytes_accessed=40 * 2**20, transcendentals=0),
        name="pairs",
    )(rows)
    first, last = call(
        edge_tiles_kernel,
        "edge_tiles",
        (shape((TILE, feature_cols), bf16), shape((TILE, feature_cols), bf16)),
        [],
        4 * TILE * atom_rows * feature_cols,
        arrival_live,
        received,
    )
    low, high = from_sides(first, last)
    radial = radial_weights.reshape(-1, channels)
    common = (radial, mix_weight, self_weight, readout.reshape(1, -1))
    tile_flops = 4 * orders * TILE * WINDOW * channels * 25
    held = functools.partial(pltpu.with_memory_space_constraint, memory_space=pltpu.VMEM)
    distant = functools.partial(pltpu.with_memory_space_constraint, memory_space=pltpu.HBM)

    def scratch(count):
        return [
            pltpu.VMEM((PATHS, orders * SUB, channels), bf16),
            pltpu.VMEM((HARM, TILE, channels), f32),
            pltpu.VMEM((HARM, TILE, channels), bf16),
            pltpu.VMEM((count, subs, HARM, stack, WINDOW), bf16),
            pltpu.VMEM((count, subs, stack, WINDOW), f32),
            pltpu.VMEM((count, subs, stack, WINDOW), f32),
        ]

    feat, inner_new, inner_energy, inner_force = call(
        functools.partial(inner_kernel, orders=orders),
        "inner",
        (
            HELD((atom_rows, feature_cols), bf16),
            HELD((inner, TILE, channels), bf16),
            HELD((inner, 1, TILE), f32),
            HELD((8, atom_rows), f32),
        ),
        [pltpu.VMEM((feature_cols, atom_rows), bf16), pltpu.VMEM((atom_rows, 8), f32)]
        + scratch(inner)
        + [pltpu.SemaphoreType.DMA((inner, subs)), pltpu.SemaphoreType.DMA((inner, 2))],
        inner * tile_flops,
        arrival_live,
        received,
        rows,
        distant(edges),
        distant(values),
        distant(changes),
        gains,
        *common,
        distant=(3, 4, 5),
    )
    new_rows, energies, forces = call(
        functools.partial(outer_kernel, orders=orders),
        "outer",
        (
            shape((atom_rows, channels), bf16),
            shape((1, atom_rows), f32),
            shape((8, atom_rows), f32),
        ),
        [
            pltpu.VMEM((4 * TILE, feature_cols), bf16),
            pltpu.VMEM((feature_cols, 4 * TILE), bf16),
            pltpu.VMEM((8, 4 * TILE), f32),
            pltpu.VMEM((4 * TILE, 8), f32),
        ]
        + scratch(2)
        + [pltpu.VMEM((2, 8, WINDOW), f32)],
        2 * tile_flops,
        low,
        high,
        held(feat),
        low_rows,
        rows,
        high_rows,
        table,
        *common,
        held(inner_new),
        held(inner_energy),
        held(inner_force),
    )
    return (energies.reshape(atom_rows), forces[:3].T, new_rows)


def solution(mesh):
    placed = (
        P(("dom", "blk"), None),
        P(("dom", "blk")),
        P(("dom", "blk"), None),
        P(("dom", "blk")),
        P(("dom", "blk")),
        P(("dom", "blk"), None),
        P(),
        P(),
        P(),
        P(),
        P(),
    )
    return jax.shard_map(
        per_device,
        mesh=mesh,
        in_specs=placed,
        out_specs=(P(("dom", "blk")), P(("dom", "blk"), None), P(("dom", "blk"), None)),
        check_vma=False,
    )
```

```python
import functools
import math

import jax
import jax.numpy as jnp
import numpy as np
from jax import lax
from jax.experimental import pallas as pl
from jax.experimental.pallas import tpu as pltpu
from jax.sharding import PartitionSpec as P

BLOCK = 64
TILE = 2 * BLOCK
WINDOW = 4 * BLOCK
SUB = BLOCK
HARM = 9
PATHS = 7
ROOT_THREE = math.sqrt(3.0)
AXES = ("dom", "blk")
VMEM_BYTES = 48 * 1024 * 1024
HELD = pltpu.VMEM


def degree(k):
    return 0 if k == 0 else (1 if k < 4 else 2)


def polynomial(square, coefficients):
    total = jnp.full_like(square, coefficients[-1])
    for value in coefficients[-2::-1]:
        total = total * square + value
    return total


SINE = [(-1.0) ** m * math.pi ** (2 * m + 1) / math.factorial(2 * m + 1) for m in range(6)]
COSINE = [(-1.0) ** m * math.pi ** (2 * m) / math.factorial(2 * m) for m in range(7)]


def solid(x, y, z):
    return [
        None,
        x,
        y,
        z,
        ROOT_THREE * x * y,
        ROOT_THREE * y * z,
        z * z - 0.5 * (x * x + y * y),
        ROOT_THREE * z * x,
        (0.5 * ROOT_THREE) * (x * x - y * y),
    ]


def chosen_rows(wanted, rows):
    source = lax.broadcasted_iota(jnp.int32, (wanted.shape[0], rows), 1)
    return (wanted == source).astype(jnp.float32).astype(jnp.bfloat16)


def as_column(row_ref):
    return jnp.transpose(jnp.broadcast_to(row_ref[...], (8, row_ref.shape[1])))[:, 0:1]


def edge_tiles_kernel(arrival_ref, received_ref, first_ref, last_ref):
    rows = received_ref.shape[0]
    wanted = as_column(arrival_ref)
    both = jnp.concatenate([wanted[0:TILE], wanted[rows - TILE :]], axis=0)
    found = jnp.dot(
        chosen_rows(both, rows), received_ref[...], preferred_element_type=jnp.float32
    ).astype(jnp.bfloat16)
    first_ref[...] = found[0:TILE]
    last_ref[...] = found[TILE:]


def pair_factors(base, rows_ref, cols_ref, edge_at, value_at, change_at, orders):
    window = pl.ds(base, WINDOW)
    for sub in range(TILE // SUB):
        half = sub * SUB // BLOCK
        here = pl.ds(pl.multiple_of(base + (BLOCK + sub * SUB), SUB), SUB)
        column = lax.broadcasted_iota(jnp.int32, (SUB, WINDOW), 1)
        row = lax.broadcasted_iota(jnp.int32, (SUB, WINDOW), 0) + (sub * SUB + BLOCK)
        offset = column - half * BLOCK
        low = jnp.where((offset >= 0) & (offset < BLOCK), cols_ref[here, 5:6], 0.0)
        high = jnp.where(
            (offset >= 2 * BLOCK) & (offset < 3 * BLOCK), cols_ref[here, 6:7], low
        )
        same = (offset >= BLOCK) & (offset < 2 * BLOCK) & (row != column)
        keep = jnp.where(same, 1.0, high)
        x, y, z = [rows_ref[a : a + 1, window] - cols_ref[here, a : a + 1] for a in range(3)]
        spread = x * x + y * y + z * z
        room = jnp.maximum(1.0 - spread, 0.0)
        squared = room * room * keep
        envelope = squared * room
        slope = -3.0 * squared
        shifted = jnp.minimum(spread, 1.0) - 0.5
        shifted_sq = shifted * shifted
        cosine = -shifted * polynomial(shifted_sq, SINE)
        sine = polynomial(shifted_sq, COSINE)
        twice = 2.0 * cosine
        cos_prev, cos_now = jnp.ones_like(cosine), cosine
        sin_prev, sin_now = jnp.zeros_like(sine), sine
        harm = solid(x, y, z)
        for n in range(orders):
            rows = slice(n * SUB, (n + 1) * SUB)
            if n == 0:
                value, change = envelope, slope
            else:
                value = envelope * cos_now
                change = slope * cos_now - (n * math.pi) * (envelope * sin_now)
            value_at[sub, rows, :] = value
            change_at[sub, rows, :] = change
            for k in range(HARM):
                edge = value if k == 0 else value * harm[k]
                edge_at[sub, k, rows, :] = edge.astype(jnp.bfloat16)
            if n >= 1:
                cos_prev, cos_now = cos_now, twice * cos_now - cos_prev
                sin_prev, sin_now = sin_now, twice * sin_now - sin_prev


def pairs_kernel(rows_ref, edge_ref, value_ref, change_ref, cols_ref, orders):
    tile = pl.program_id(0)

    @pl.when(tile == 0)
    def _():
        cols_ref[...] = jnp.transpose(rows_ref[...])

    base = pl.multiple_of(tile * TILE, TILE)
    pair_factors(
        base, rows_ref, cols_ref, edge_ref.at[0], value_ref.at[0], change_ref.at[0], orders
    )


def spread_weights(radial_ref, narrow_ref, orders):
    for path in range(PATHS):
        for n in range(orders):
            row = radial_ref[n * PATHS + path : n * PATHS + path + 1, :]
            narrow_ref[path, n * SUB : (n + 1) * SUB, :] = jnp.broadcast_to(
                row, (SUB, row.shape[1])
            ).astype(jnp.bfloat16)


def fetch(sources, held):
    edge_hbm, value_hbm, change_hbm = sources
    edge_ref, value_ref, change_ref, edge_sem, factor_sem = held
    count, subs = edge_ref.shape[:2]

    def edges(at, sub):
        return pltpu.make_async_copy(
            edge_hbm.at[at, sub], edge_ref.at[at, sub], edge_sem.at[at, sub]
        )

    def factors(at):
        return (
            pltpu.make_async_copy(value_hbm.at[at], value_ref.at[at], factor_sem.at[at, 0]),
            pltpu.make_async_copy(change_hbm.at[at], change_ref.at[at], factor_sem.at[at, 1]),
        )

    for at in range(count):
        for sub in range(subs):
            edges(at, sub).start()
        for copy in factors(at):
            copy.start()
    return edges, factors


def one_tile(at, base, refs, gain_of, copies, results, orders):
    feat_ref, turned_ref, rows_ref, cols_ref, edge_ref, value_ref, change_ref = refs[:7]
    radial_ref, narrow_ref, mix_ref, self_ref, readout_ref = refs[7:12]
    message_ref, grad_ref = refs[12:]
    channels = mix_ref.shape[0]
    window = pl.ds(base, WINDOW)
    centre = pl.ds(pl.multiple_of(base + BLOCK, BLOCK), TILE)
    subs = range(TILE // SUB)

    def weight(n, path):
        return radial_ref[n * PATHS + path : n * PATHS + path + 1, :]

    def piece(k):
        return feat_ref[window, k * channels : (k + 1) * channels]

    def path_sum(product, first, path):
        total = None
        for n in range(orders):
            part = product[n * SUB : (n + 1) * SUB, first : first + channels] * weight(n, path)
            total = part if total is None else total + part
        return total

    for sub in subs:
        rows = slice(sub * SUB, (sub + 1) * SUB)
        if copies is not None:
            copies[0](at, sub).wait()
        for k in range(0, HARM, 2):
            last = min(k + 2, HARM)
            pairs = jnp.dot(
                edge_ref[at, sub, 0],
                feat_ref[window, k * channels : last * channels],
                preferred_element_type=jnp.float32,
            )
            for which in range(k, last):
                path = 0 if which == 0 else 2 + degree(which)
                message_ref[which, rows, :] = path_sum(pairs, (which - k) * channels, path)
        for k in range(1, HARM):
            both = jnp.concatenate([piece(k), piece(0)], axis=1)
            pairs = jnp.dot(edge_ref[at, sub, k], both, preferred_element_type=jnp.float32)
            message_ref[0, rows, :] += path_sum(pairs, 0, 4 + degree(k))
            message_ref[k, rows, :] += path_sum(pairs, channels, degree(k))

    gain = gain_of(centre)
    zero = message_ref[0]
    first = sum(message_ref[k] * message_ref[k] for k in range(1, 4))
    second = sum(message_ref[k] * message_ref[k] for k in range(4, HARM))
    basis = zero + gain[0] * (zero * zero) + gain[1] * first + gain[2] * second
    live = cols_ref[centre, 3:4]
    mixed = jnp.dot(
        basis.astype(jnp.bfloat16), mix_ref[...], preferred_element_type=jnp.float32
    ) + jnp.dot(feat_ref[centre, 0:channels], self_ref[...], preferred_element_type=jnp.float32)
    gate = 1.0 / (1.0 + jnp.exp(-mixed))
    silu = mixed * gate
    readout = readout_ref[...]
    fresh = (live * mixed).astype(jnp.bfloat16)
    energy = jnp.sum(jnp.transpose(live * (readout * silu)), axis=0, keepdims=True)
    mixed_grad = live * readout * (gate * (1.0 + mixed - silu))
    basis_grad = lax.dot_general(
        mixed_grad.astype(jnp.bfloat16),
        mix_ref[...],
        (((1,), (1,)), ((), ())),
        preferred_element_type=jnp.float32,
    )
    grad_ref[0] = (basis_grad * (1.0 + 2.0 * gain[0] * zero)).astype(jnp.bfloat16)
    for k in range(1, HARM):
        grad_ref[k] = (basis_grad * (2.0 * gain[degree(k)]) * message_ref[k]).astype(jnp.bfloat16)

    def backward(sub):
        rows = slice(sub * SUB, (sub + 1) * SUB)
        here = pl.ds(pl.multiple_of(base + (BLOCK + sub * SUB), SUB), SUB)
        grads = [jnp.concatenate([grad_ref[k, rows, :]] * orders, axis=0) for k in range(HARM)]
        x, y, z = [rows_ref[a : a + 1, window] - cols_ref[here, a : a + 1] for a in range(3)]
        harm = solid(x, y, z)
        root_x, root_y, root_z = ROOT_THREE * x, ROOT_THREE * y, ROOT_THREE * z
        slopes = {
            1: {0: None},
            2: {1: None},
            3: {2: None},
            4: {0: root_y, 1: root_x},
            5: {1: root_z, 2: root_y},
            6: {0: -x, 1: -y, 2: 2.0 * z},
            7: {0: root_z, 2: root_x},
            8: {0: root_x, 1: -root_y},
        }

        def over_orders(cross, factor_ref):
            total = None
            for n in range(orders):
                part = cross[n * SUB : (n + 1) * SUB] * factor_ref[
                    at, sub, n * SUB : (n + 1) * SUB, :
                ]
                total = part if total is None else total + part
            return total

        left = jnp.concatenate(
            [grads[k] * narrow_ref[0 if k == 0 else 2 + degree(k)] for k in range(HARM)], axis=1
        )
        cross = jnp.dot(left, turned_ref[:, window], preferred_element_type=jnp.float32)
        radial_total = over_orders(cross, change_ref)
        pull = [None, None, None]
        for k in range(1, HARM):
            left = jnp.concatenate(
                [grads[0] * narrow_ref[4 + degree(k)], grads[k] * narrow_ref[degree(k)]], axis=1
            )
            both = jnp.concatenate(
                [
                    turned_ref[k * channels : (k + 1) * channels, window],
                    turned_ref[0:channels, window],
                ],
                axis=0,
            )
            cross = jnp.dot(left, both, preferred_element_type=jnp.float32)
            along = over_orders(cross, value_ref)
            radial_total = radial_total + over_orders(cross, change_ref) * harm[k]
            for axis, factor in slopes[k].items():
                term = along if factor is None else along * factor
                pull[axis] = term if pull[axis] is None else pull[axis] + term
        radial_total = 2.0 * radial_total
        return [pull[axis] + delta * radial_total for axis, delta in enumerate((x, y, z))]

    if copies is not None:
        for copy in copies[1](at):
            copy.wait()
    onto_window = [None, None, None]
    columns_out = [[], [], []]
    for sub in subs:
        for axis, total in enumerate(backward(sub)):
            summed = jnp.sum(total, axis=0, keepdims=True)
            onto_window[axis] = summed if sub == 0 else onto_window[axis] + summed
            columns_out[axis].append(jnp.sum(total, axis=1, keepdims=True))
    lane = lax.broadcasted_iota(jnp.int32, (TILE, 8), 1)
    row = lax.broadcasted_iota(jnp.int32, (8, WINDOW), 0)
    packed = jnp.zeros((TILE, 8), jnp.float32)
    pulled = jnp.zeros((8, WINDOW), jnp.float32)
    for axis in range(3):
        packed = jnp.where(lane == axis, jnp.concatenate(columns_out[axis], axis=0), packed)
        pulled = jnp.where(row == axis, onto_window[axis], pulled)
    turned = jnp.transpose(packed)
    side = jnp.zeros((8, BLOCK), jnp.float32)
    results(fresh, energy, jnp.concatenate([side, turned, side], axis=1) - pulled)


def inner_kernel(
    arrival_ref,
    received_ref,
    first_ref,
    last_ref,
    rows_ref,
    edge_hbm,
    value_hbm,
    change_hbm,
    gains_ref,
    radial_ref,
    mix_ref,
    self_ref,
    readout_ref,
    feat_ref,
    new_ref,
    energy_ref,
    force_ref,
    turned_ref,
    cols_ref,
    narrow_ref,
    message_ref,
    grad_ref,
    edge_ref,
    value_ref,
    change_ref,
    edge_sem,
    factor_sem,
    orders,
):
    held = (edge_ref, value_ref, change_ref, edge_sem, factor_sem)
    copies = fetch((edge_hbm, value_hbm, change_hbm), held)
    rows = received_ref.shape[0]
    channels = mix_ref.shape[0]
    wanted = as_column(arrival_ref)
    cols_ref[...] = jnp.transpose(rows_ref[...])
    spread_weights(radial_ref, narrow_ref, orders)
    force_ref[...] = jnp.zeros_like(force_ref)
    feat_ref[0:TILE, :] = first_ref[...]
    turned_ref[:, 0:TILE] = jnp.transpose(first_ref[...])
    for part in range(1, rows // TILE - 1):
        here = slice(part * TILE, (part + 1) * TILE)
        found = jnp.dot(
            chosen_rows(wanted[here], rows),
            received_ref[...],
            preferred_element_type=jnp.float32,
        ).astype(jnp.bfloat16)
        feat_ref[here, :] = found
        turned_ref[:, here] = jnp.transpose(found)
    feat_ref[rows - TILE :, :] = last_ref[...]
    turned_ref[:, rows - TILE :] = jnp.transpose(last_ref[...])
    refs = (feat_ref, turned_ref, rows_ref, cols_ref, edge_ref, value_ref, change_ref)
    refs += (radial_ref, narrow_ref, mix_ref, self_ref, readout_ref, message_ref, grad_ref)

    def gain_of(centre):
        return [gains_ref[centre, l * channels : (l + 1) * channels] for l in range(3)]

    def body(at, carry):
        base = pl.multiple_of(at * TILE, TILE)

        def results(fresh, energy, force):
            new_ref[at] = fresh
            energy_ref[at] = energy
            force_ref[:, pl.ds(base, WINDOW)] += force

        one_tile(at, base, refs, gain_of, copies, results, orders)
        return carry

    for at in range(edge_hbm.shape[0]):
        body(at, 0)


def outer_kernel(
    low_ref,
    high_ref,
    feat_ref,
    low_rows_ref,
    rows_ref,
    high_rows_ref,
    table_ref,
    radial_ref,
    mix_ref,
    self_ref,
    readout_ref,
    inner_new_ref,
    inner_energy_ref,
    inner_force_ref,
    new_ref,
    energy_ref,
    force_ref,
    near_ref,
    turned_ref,
    near_rows_ref,
    cols_ref,
    narrow_ref,
    message_ref,
    grad_ref,
    edge_ref,
    value_ref,
    change_ref,
    total_ref,
    orders,
):
    rows = feat_ref.shape[0]
    channels = mix_ref.shape[0]
    near_rows_ref[:, 0:TILE] = low_rows_ref[...]
    near_rows_ref[:, TILE : 2 * TILE] = rows_ref[:, 0:TILE]
    near_rows_ref[:, 2 * TILE : 3 * TILE] = rows_ref[:, rows - TILE :]
    near_rows_ref[:, 3 * TILE :] = high_rows_ref[...]
    cols_ref[...] = jnp.transpose(near_rows_ref[...])
    spread_weights(radial_ref, narrow_ref, orders)
    near_ref[0:TILE, :] = low_ref[...]
    near_ref[TILE : 2 * TILE, :] = feat_ref[0:TILE, :]
    near_ref[2 * TILE : 3 * TILE, :] = feat_ref[rows - TILE :, :]
    near_ref[3 * TILE :, :] = high_ref[...]
    for part in range(4):
        here = slice(part * TILE, (part + 1) * TILE)
        turned_ref[:, here] = jnp.transpose(near_ref[here, :])
    refs = (near_ref, turned_ref, near_rows_ref, cols_ref, edge_ref, value_ref, change_ref)
    refs += (radial_ref, narrow_ref, mix_ref, self_ref, readout_ref, message_ref, grad_ref)

    def gain_of(centre):
        kinds = lax.broadcasted_iota(jnp.int32, (TILE, table_ref.shape[0]), 1)
        picked = (cols_ref[centre, 4:5].astype(jnp.int32) == kinds).astype(jnp.float32)
        rows_of = jnp.dot(
            picked,
            table_ref[...],
            precision=lax.Precision.HIGHEST,
            preferred_element_type=jnp.float32,
        )
        return [rows_of[:, l * channels : (l + 1) * channels] for l in range(3)]

    def body(at, carry):
        base = pl.multiple_of(at * WINDOW, WINDOW)

        def results(fresh, energy, force):
            total_ref[at] = force

            if at == 0:
                new_ref[0:BLOCK, :] = fresh[BLOCK:, :]
                energy_ref[:, 0:BLOCK] = energy[:, BLOCK:]

            if at == 1:
                new_ref[rows - BLOCK :, :] = fresh[0:BLOCK, :]
                energy_ref[:, rows - BLOCK :] = energy[:, 0:BLOCK]

        pair_factors(
            base, near_rows_ref, cols_ref, edge_ref.at[at], value_ref.at[at], change_ref.at[at], orders
        )
        one_tile(at, base, refs, gain_of, None, results, orders)
        return carry

    for at in range(2):
        body(at, 0)
    inner = inner_new_ref.shape[0]
    for at in range(inner):
        here = slice(BLOCK + at * TILE, BLOCK + (at + 1) * TILE)
        new_ref[here, :] = inner_new_ref[at]
        energy_ref[:, here] = inner_energy_ref[at]
    force_ref[...] = inner_force_ref[0:3, :]
    force_ref[:, 0:TILE] += total_ref[0, 0:3, TILE:]
    force_ref[:, rows - TILE :] += total_ref[1, 0:3, 0:TILE]


def call(kernel, name, out_shape, scratch, flops, *operands, distant=()):
    whole = pl.BlockSpec(memory_space=pltpu.VMEM)
    hbm = pl.BlockSpec(memory_space=pl.ANY)
    return pl.pallas_call(
        kernel,
        out_shape=out_shape,
        in_specs=[hbm if at in distant else whole for at in range(len(operands))],
        out_specs=jax.tree.map(lambda _: whole, out_shape),
        scratch_shapes=scratch,
        compiler_params=pltpu.CompilerParams(vmem_limit_bytes=VMEM_BYTES),
        cost_estimate=pl.CostEstimate(flops=flops, bytes_accessed=4 * 2**20, transcendentals=0),
        name=name,
    )(*operands)


def from_sides(block_low, block_high):
    count = lax.axis_size(AXES)
    forward = [(i, i + 1) for i in range(count - 1)]
    backward = [(target, source) for source, target in forward]
    low = lax.ppermute(block_high, AXES, forward)
    high = lax.ppermute(block_low, AXES, backward)
    return low, high


def per_device(
    features_domain,
    arrival,
    positions,
    species,
    block_count,
    pair_block,
    radial_weights,
    species_weights,
    mix_weight,
    self_weight,
    readout,
):
    devices = lax.axis_size(AXES)
    atom_rows, feature_cols = features_domain.shape
    piece_rows = atom_rows // devices
    parcels = features_domain.reshape(devices, piece_rows, feature_cols)
    received = lax.all_to_all(parcels, AXES, split_axis=0, concat_axis=0, tiled=True)
    received = received.reshape(atom_rows, feature_cols)
    blocks = block_count.shape[0]
    bf16, f32 = jnp.bfloat16, jnp.float32
    shape = jax.ShapeDtypeStruct

    def per_slot(values):
        return jnp.broadcast_to(values[:, None], (blocks, BLOCK)).reshape(1, atom_rows)

    slot = jnp.arange(BLOCK, dtype=jnp.int32)
    live = (slot[None, :] < block_count[:, None]).reshape(1, atom_rows)
    arrival_live = jnp.where(live, arrival.reshape(1, atom_rows), -1)
    listed = (pair_block >= 0).astype(f32)
    rows = jnp.concatenate(
        [
            positions.T,
            live.astype(f32),
            species.astype(f32).reshape(1, atom_rows),
            per_slot(listed[:, 0]),
            per_slot(listed[:, 2]),
            jnp.zeros((1, atom_rows), f32),
        ],
        axis=0,
    )
    low_rows, high_rows = from_sides(rows[:, :TILE], rows[:, atom_rows - TILE :])
    species_total = species_weights.shape[0]
    one_hot = (species[:, None] == jnp.arange(species_total, dtype=jnp.int32)[None, :]).astype(f32)
    table = species_weights.reshape(species_total, -1)
    gains = jnp.dot(one_hot, table, precision=lax.Precision.HIGHEST)
    orders, _, channels = radial_weights.shape
    inner = atom_rows // TILE - 1
    subs = TILE // SUB
    stack = orders * SUB
    edges, values, changes = pl.pallas_call(
        functools.partial(pairs_kernel, orders=orders),
        grid=(inner,),
        out_shape=(
            pltpu.HBM((inner, subs, HARM, stack, WINDOW), bf16),
            pltpu.HBM((inner, subs, stack, WINDOW), f32),
            pltpu.HBM((inner, subs, stack, WINDOW), f32),
        ),
        in_specs=[pl.BlockSpec((8, atom_rows), lambda t: (0, 0))],
        out_specs=(
            pl.BlockSpec((1, subs, HARM, stack, WINDOW), lambda t: (t, 0, 0, 0, 0)),
            pl.BlockSpec((1, subs, stack, WINDOW), lambda t: (t, 0, 0, 0)),
            pl.BlockSpec((1, subs, stack, WINDOW), lambda t: (t, 0, 0, 0)),
        ),
        scratch_shapes=[pltpu.VMEM((atom_rows, 8), f32)],
        compiler_params=pltpu.CompilerParams(vmem_limit_bytes=VMEM_BYTES),
        cost_estimate=pl.CostEstimate(flops=10**10, bytes_accessed=40 * 2**20, transcendentals=0),
        name="pairs",
    )(rows)
    first, last = call(
        edge_tiles_kernel,
        "edge_tiles",
        (shape((TILE, feature_cols), bf16), shape((TILE, feature_cols), bf16)),
        [],
        4 * TILE * atom_rows * feature_cols,
        arrival_live,
        received,
    )
    low, high = from_sides(first, last)
    radial = radial_weights.reshape(-1, channels)
    common = (radial, mix_weight, self_weight, readout.reshape(1, -1))
    tile_flops = 4 * orders * TILE * WINDOW * channels * 25
    held = functools.partial(pltpu.with_memory_space_constraint, memory_space=pltpu.VMEM)
    distant = functools.partial(pltpu.with_memory_space_constraint, memory_space=pltpu.HBM)

    def scratch(count):
        return [
            pltpu.VMEM((PATHS, orders * SUB, channels), bf16),
            pltpu.VMEM((HARM, TILE, channels), f32),
            pltpu.VMEM((HARM, TILE, channels), bf16),
            pltpu.VMEM((count, subs, HARM, stack, WINDOW), bf16),
            pltpu.VMEM((count, subs, stack, WINDOW), f32),
            pltpu.VMEM((count, subs, stack, WINDOW), f32),
        ]

    feat, inner_new, inner_energy, inner_force = call(
        functools.partial(inner_kernel, orders=orders),
        "inner",
        (
            HELD((atom_rows, feature_cols), bf16),
            HELD((inner, TILE, channels), bf16),
            HELD((inner, 1, TILE), f32),
            HELD((8, atom_rows), f32),
        ),
        [pltpu.VMEM((feature_cols, atom_rows), bf16), pltpu.VMEM((atom_rows, 8), f32)]
        + scratch(inner)
        + [pltpu.SemaphoreType.DMA((inner, subs)), pltpu.SemaphoreType.DMA((inner, 2))],
        inner * tile_flops,
        arrival_live,
        received,
        first,
        last,
        rows,
        distant(edges),
        distant(values),
        distant(changes),
        gains,
        *common,
        distant=(5, 6, 7),
    )
    new_rows, energies, forces = call(
        functools.partial(outer_kernel, orders=orders),
        "outer",
        (
            shape((atom_rows, channels), bf16),
            shape((1, atom_rows), f32),
            shape((3, atom_rows), f32),
        ),
        [
            pltpu.VMEM((4 * TILE, feature_cols), bf16),
            pltpu.VMEM((feature_cols, 4 * TILE), bf16),
            pltpu.VMEM((8, 4 * TILE), f32),
            pltpu.VMEM((4 * TILE, 8), f32),
        ]
        + scratch(2)
        + [pltpu.VMEM((2, 8, WINDOW), f32)],
        2 * tile_flops,
        low,
        high,
        held(feat),
        low_rows,
        rows,
        high_rows,
        table,
        *common,
        held(inner_new),
        held(inner_energy),
        held(inner_force),
    )
    return (energies.reshape(atom_rows), forces.T, new_rows)


def solution(mesh):
    placed = (
        P(("dom", "blk"), None),
        P(("dom", "blk")),
        P(("dom", "blk"), None),
        P(("dom", "blk")),
        P(("dom", "blk")),
        P(("dom", "blk"), None),
        P(),
        P(),
        P(),
        P(),
        P(),
    )
    return jax.shard_map(
        per_device,
        mesh=mesh,
        in_specs=placed,
        out_specs=(P(("dom", "blk")), P(("dom", "blk"), None), P(("dom", "blk"), None)),
        check_vma=False,
    )
```

```python
import functools
import math

import jax
import jax.numpy as jnp
import numpy as np
from jax import lax
from jax.experimental import pallas as pl
from jax.experimental.pallas import tpu as pltpu
from jax.sharding import PartitionSpec as P

BLOCK = 64
TILE = 2 * BLOCK
WINDOW = 4 * BLOCK
SUB = BLOCK
HARM = 9
PATHS = 7
ROOT_THREE = math.sqrt(3.0)
AXES = ("dom", "blk")
VMEM_BYTES = 48 * 1024 * 1024
HELD = pltpu.VMEM


def degree(k):
    return 0 if k == 0 else (1 if k < 4 else 2)


def polynomial(square, coefficients):
    total = jnp.full_like(square, coefficients[-1])
    for value in coefficients[-2::-1]:
        total = total * square + value
    return total


SINE = [(-1.0) ** m * math.pi ** (2 * m + 1) / math.factorial(2 * m + 1) for m in range(6)]
COSINE = [(-1.0) ** m * math.pi ** (2 * m) / math.factorial(2 * m) for m in range(7)]


def solid(x, y, z):
    return [
        None,
        x,
        y,
        z,
        ROOT_THREE * x * y,
        ROOT_THREE * y * z,
        z * z - 0.5 * (x * x + y * y),
        ROOT_THREE * z * x,
        (0.5 * ROOT_THREE) * (x * x - y * y),
    ]


def chosen_rows(wanted, rows):
    source = lax.broadcasted_iota(jnp.int32, (wanted.shape[0], rows), 1)
    return (wanted == source).astype(jnp.float32).astype(jnp.bfloat16)


def as_column(row_ref):
    return jnp.transpose(jnp.broadcast_to(row_ref[...], (8, row_ref.shape[1])))[:, 0:1]


def edge_tiles_kernel(arrival_ref, received_ref, first_ref, last_ref):
    rows = received_ref.shape[0]
    wanted = as_column(arrival_ref)
    both = jnp.concatenate([wanted[0:TILE], wanted[rows - TILE :]], axis=0)
    found = jnp.dot(
        chosen_rows(both, rows), received_ref[...], preferred_element_type=jnp.float32
    ).astype(jnp.bfloat16)
    first_ref[...] = found[0:TILE]
    last_ref[...] = found[TILE:]


def pair_factors(base, rows_ref, cols_ref, edge_at, value_at, change_at, orders):
    window = pl.ds(base, WINDOW)
    for sub in range(TILE // SUB):
        half = sub * SUB // BLOCK
        here = pl.ds(pl.multiple_of(base + (BLOCK + sub * SUB), SUB), SUB)
        column = lax.broadcasted_iota(jnp.int32, (SUB, WINDOW), 1)
        row = lax.broadcasted_iota(jnp.int32, (SUB, WINDOW), 0) + (sub * SUB + BLOCK)
        offset = column - half * BLOCK
        low = jnp.where((offset >= 0) & (offset < BLOCK), cols_ref[here, 5:6], 0.0)
        high = jnp.where(
            (offset >= 2 * BLOCK) & (offset < 3 * BLOCK), cols_ref[here, 6:7], low
        )
        same = (offset >= BLOCK) & (offset < 2 * BLOCK) & (row != column)
        keep = jnp.where(same, 1.0, high)
        x, y, z = [rows_ref[a : a + 1, window] - cols_ref[here, a : a + 1] for a in range(3)]
        spread = x * x + y * y + z * z
        room = jnp.maximum(1.0 - spread, 0.0)
        squared = room * room * keep
        envelope = squared * room
        slope = -3.0 * squared
        shifted = jnp.minimum(spread, 1.0) - 0.5
        shifted_sq = shifted * shifted
        cosine = -shifted * polynomial(shifted_sq, SINE)
        sine = polynomial(shifted_sq, COSINE)
        twice = 2.0 * cosine
        cos_prev, cos_now = jnp.ones_like(cosine), cosine
        sin_prev, sin_now = jnp.zeros_like(sine), sine
        harm = solid(x, y, z)
        for n in range(orders):
            rows = slice(n * SUB, (n + 1) * SUB)
            if n == 0:
                value, change = envelope, slope
            else:
                value = envelope * cos_now
                change = slope * cos_now - (n * math.pi) * (envelope * sin_now)
            value_at[sub, rows, :] = value.astype(jnp.bfloat16)
            change_at[sub, rows, :] = change.astype(jnp.bfloat16)
            for k in range(HARM):
                edge = value if k == 0 else value * harm[k]
                edge_at[sub, k, rows, :] = edge.astype(jnp.bfloat16)
            if n >= 1:
                cos_prev, cos_now = cos_now, twice * cos_now - cos_prev
                sin_prev, sin_now = sin_now, twice * sin_now - sin_prev


def pairs_kernel(rows_ref, edge_ref, value_ref, change_ref, cols_ref, orders):
    tile = pl.program_id(0)

    @pl.when(tile == 0)
    def _():
        cols_ref[...] = jnp.transpose(rows_ref[...])

    base = pl.multiple_of(tile * TILE, TILE)
    pair_factors(
        base, rows_ref, cols_ref, edge_ref.at[0], value_ref.at[0], change_ref.at[0], orders
    )


def spread_weights(radial_ref, narrow_ref, orders):
    for path in range(PATHS):
        for n in range(orders):
            row = radial_ref[n * PATHS + path : n * PATHS + path + 1, :]
            narrow_ref[path, n * SUB : (n + 1) * SUB, :] = jnp.broadcast_to(
                row, (SUB, row.shape[1])
            ).astype(jnp.bfloat16)


def fetch(sources, held):
    edge_hbm, value_hbm, change_hbm = sources
    edge_ref, value_ref, change_ref, edge_sem, factor_sem = held
    count, subs = edge_ref.shape[:2]

    def edges(at, sub):
        return pltpu.make_async_copy(
            edge_hbm.at[at, sub], edge_ref.at[at, sub], edge_sem.at[at, sub]
        )

    def factors(at):
        return (
            pltpu.make_async_copy(value_hbm.at[at], value_ref.at[at], factor_sem.at[at, 0]),
            pltpu.make_async_copy(change_hbm.at[at], change_ref.at[at], factor_sem.at[at, 1]),
        )

    for at in range(count):
        for sub in range(subs):
            edges(at, sub).start()
        for copy in factors(at):
            copy.start()
    return edges, factors


def one_tile(at, base, refs, gain_of, copies, results, orders):
    feat_ref, turned_ref, rows_ref, cols_ref, edge_ref, value_ref, change_ref = refs[:7]
    radial_ref, narrow_ref, mix_ref, self_ref, readout_ref = refs[7:12]
    message_ref, grad_ref = refs[12:]
    channels = mix_ref.shape[0]
    window = pl.ds(base, WINDOW)
    centre = pl.ds(pl.multiple_of(base + BLOCK, BLOCK), TILE)
    subs = range(TILE // SUB)

    def weight(n, path):
        return radial_ref[n * PATHS + path : n * PATHS + path + 1, :]

    def piece(k):
        return feat_ref[window, k * channels : (k + 1) * channels]

    def path_sum(product, first, path):
        total = None
        for n in range(orders):
            part = product[n * SUB : (n + 1) * SUB, first : first + channels] * weight(n, path)
            total = part if total is None else total + part
        return total

    for sub in subs:
        rows = slice(sub * SUB, (sub + 1) * SUB)
        if copies is not None:
            copies[0](at, sub).wait()
        found = {}
        for k in range(0, HARM, 2):
            last = min(k + 2, HARM)
            pairs = jnp.dot(
                edge_ref[at, sub, 0],
                feat_ref[window, k * channels : last * channels],
                preferred_element_type=jnp.float32,
            )
            for which in range(k, last):
                path = 0 if which == 0 else 2 + degree(which)
                found[which] = path_sum(pairs, (which - k) * channels, path)
        for k in range(1, HARM):
            both = jnp.concatenate([piece(k), piece(0)], axis=1)
            pairs = jnp.dot(edge_ref[at, sub, k], both, preferred_element_type=jnp.float32)
            found[0] = found[0] + path_sum(pairs, 0, 4 + degree(k))
            message_ref[k, rows, :] = found[k] + path_sum(pairs, channels, degree(k))
        message_ref[0, rows, :] = found[0]

    gain = gain_of(centre)
    zero = message_ref[0]
    first = sum(message_ref[k] * message_ref[k] for k in range(1, 4))
    second = sum(message_ref[k] * message_ref[k] for k in range(4, HARM))
    basis = zero + gain[0] * (zero * zero) + gain[1] * first + gain[2] * second
    live = cols_ref[centre, 3:4]
    mixed = jnp.dot(
        basis.astype(jnp.bfloat16), mix_ref[...], preferred_element_type=jnp.float32
    ) + jnp.dot(feat_ref[centre, 0:channels], self_ref[...], preferred_element_type=jnp.float32)
    gate = 1.0 / (1.0 + jnp.exp(-mixed))
    silu = mixed * gate
    readout = readout_ref[...]
    fresh = (live * mixed).astype(jnp.bfloat16)
    energy = jnp.sum(jnp.transpose(live * (readout * silu)), axis=0, keepdims=True)
    mixed_grad = live * readout * (gate * (1.0 + mixed - silu))
    basis_grad = lax.dot_general(
        mixed_grad.astype(jnp.bfloat16),
        mix_ref[...],
        (((1,), (1,)), ((), ())),
        preferred_element_type=jnp.float32,
    )
    grad_ref[0] = (basis_grad * (1.0 + 2.0 * gain[0] * zero)).astype(jnp.bfloat16)
    for k in range(1, HARM):
        grad_ref[k] = (basis_grad * (2.0 * gain[degree(k)]) * message_ref[k]).astype(jnp.bfloat16)

    def backward(sub):
        rows = slice(sub * SUB, (sub + 1) * SUB)
        here = pl.ds(pl.multiple_of(base + (BLOCK + sub * SUB), SUB), SUB)
        grads = [jnp.concatenate([grad_ref[k, rows, :]] * orders, axis=0) for k in range(HARM)]
        x, y, z = [rows_ref[a : a + 1, window] - cols_ref[here, a : a + 1] for a in range(3)]
        harm = solid(x, y, z)
        root_x, root_y, root_z = ROOT_THREE * x, ROOT_THREE * y, ROOT_THREE * z
        slopes = {
            1: {0: None},
            2: {1: None},
            3: {2: None},
            4: {0: root_y, 1: root_x},
            5: {1: root_z, 2: root_y},
            6: {0: -x, 1: -y, 2: 2.0 * z},
            7: {0: root_z, 2: root_x},
            8: {0: root_x, 1: -root_y},
        }

        def over_orders(cross, factor_ref):
            parts = [
                cross[n * SUB : (n + 1) * SUB].astype(jnp.bfloat16)
                * factor_ref[at, sub, n * SUB : (n + 1) * SUB, :]
                for n in range(orders)
            ]
            while len(parts) > 1:
                parts = [parts[m] + parts[m + 1] for m in range(0, len(parts), 2)]
            return parts[0].astype(jnp.float32)

        left = jnp.concatenate(
            [grads[k] * narrow_ref[0 if k == 0 else 2 + degree(k)] for k in range(HARM)], axis=1
        )
        cross = jnp.dot(left, turned_ref[:, window], preferred_element_type=jnp.float32)
        radial_total = over_orders(cross, change_ref)
        pull = [None, None, None]
        for k in range(1, HARM):
            left = jnp.concatenate(
                [grads[0] * narrow_ref[4 + degree(k)], grads[k] * narrow_ref[degree(k)]], axis=1
            )
            both = jnp.concatenate(
                [
                    turned_ref[k * channels : (k + 1) * channels, window],
                    turned_ref[0:channels, window],
                ],
                axis=0,
            )
            cross = jnp.dot(left, both, preferred_element_type=jnp.float32)
            along = over_orders(cross, value_ref)
            radial_total = radial_total + over_orders(cross, change_ref) * harm[k]
            for axis, factor in slopes[k].items():
                term = along if factor is None else along * factor
                pull[axis] = term if pull[axis] is None else pull[axis] + term
        radial_total = 2.0 * radial_total
        return [pull[axis] + delta * radial_total for axis, delta in enumerate((x, y, z))]

    if copies is not None:
        for copy in copies[1](at):
            copy.wait()
    onto_window = [None, None, None]
    columns_out = [[], [], []]
    for sub in subs:
        for axis, total in enumerate(backward(sub)):
            summed = jnp.sum(total, axis=0, keepdims=True)
            onto_window[axis] = summed if sub == 0 else onto_window[axis] + summed
            columns_out[axis].append(jnp.sum(total, axis=1, keepdims=True))
    lane = lax.broadcasted_iota(jnp.int32, (TILE, 8), 1)
    row = lax.broadcasted_iota(jnp.int32, (8, WINDOW), 0)
    packed = jnp.zeros((TILE, 8), jnp.float32)
    pulled = jnp.zeros((8, WINDOW), jnp.float32)
    for axis in range(3):
        packed = jnp.where(lane == axis, jnp.concatenate(columns_out[axis], axis=0), packed)
        pulled = jnp.where(row == axis, onto_window[axis], pulled)
    turned = jnp.transpose(packed)
    side = jnp.zeros((8, BLOCK), jnp.float32)
    results(fresh, energy, jnp.concatenate([side, turned, side], axis=1) - pulled)


def inner_kernel(
    arrival_ref,
    received_ref,
    first_ref,
    last_ref,
    rows_ref,
    edge_hbm,
    value_hbm,
    change_hbm,
    gains_ref,
    radial_ref,
    mix_ref,
    self_ref,
    readout_ref,
    feat_ref,
    new_ref,
    energy_ref,
    force_ref,
    turned_ref,
    cols_ref,
    narrow_ref,
    message_ref,
    grad_ref,
    edge_ref,
    value_ref,
    change_ref,
    edge_sem,
    factor_sem,
    orders,
):
    held = (edge_ref, value_ref, change_ref, edge_sem, factor_sem)
    copies = fetch((edge_hbm, value_hbm, change_hbm), held)
    rows = received_ref.shape[0]
    channels = mix_ref.shape[0]
    wanted = as_column(arrival_ref)
    cols_ref[...] = jnp.transpose(rows_ref[...])
    spread_weights(radial_ref, narrow_ref, orders)
    force_ref[...] = jnp.zeros_like(force_ref)
    feat_ref[0:TILE, :] = first_ref[...]
    turned_ref[:, 0:TILE] = jnp.transpose(first_ref[...])
    for part in range(1, rows // TILE - 1):
        here = slice(part * TILE, (part + 1) * TILE)
        found = jnp.dot(
            chosen_rows(wanted[here], rows),
            received_ref[...],
            preferred_element_type=jnp.float32,
        ).astype(jnp.bfloat16)
        feat_ref[here, :] = found
        turned_ref[:, here] = jnp.transpose(found)
    feat_ref[rows - TILE :, :] = last_ref[...]
    turned_ref[:, rows - TILE :] = jnp.transpose(last_ref[...])
    refs = (feat_ref, turned_ref, rows_ref, cols_ref, edge_ref, value_ref, change_ref)
    refs += (radial_ref, narrow_ref, mix_ref, self_ref, readout_ref, message_ref, grad_ref)

    def gain_of(centre):
        return [gains_ref[centre, l * channels : (l + 1) * channels] for l in range(3)]

    def body(at, carry):
        base = pl.multiple_of(at * TILE, TILE)

        def results(fresh, energy, force):
            new_ref[at] = fresh
            energy_ref[at] = energy
            force_ref[:, pl.ds(base, WINDOW)] += force

        one_tile(at, base, refs, gain_of, copies, results, orders)
        return carry

    lax.fori_loop(0, edge_hbm.shape[0], body, 0)


def outer_kernel(
    low_ref,
    high_ref,
    feat_ref,
    low_rows_ref,
    rows_ref,
    high_rows_ref,
    table_ref,
    radial_ref,
    mix_ref,
    self_ref,
    readout_ref,
    inner_new_ref,
    inner_energy_ref,
    inner_force_ref,
    new_ref,
    energy_ref,
    force_ref,
    near_ref,
    turned_ref,
    near_rows_ref,
    cols_ref,
    narrow_ref,
    message_ref,
    grad_ref,
    edge_ref,
    value_ref,
    change_ref,
    total_ref,
    orders,
):
    rows = feat_ref.shape[0]
    channels = mix_ref.shape[0]
    near_rows_ref[:, 0:TILE] = low_rows_ref[...]
    near_rows_ref[:, TILE : 2 * TILE] = rows_ref[:, 0:TILE]
    near_rows_ref[:, 2 * TILE : 3 * TILE] = rows_ref[:, rows - TILE :]
    near_rows_ref[:, 3 * TILE :] = high_rows_ref[...]
    cols_ref[...] = jnp.transpose(near_rows_ref[...])
    spread_weights(radial_ref, narrow_ref, orders)
    near_ref[0:TILE, :] = low_ref[...]
    near_ref[TILE : 2 * TILE, :] = feat_ref[0:TILE, :]
    near_ref[2 * TILE : 3 * TILE, :] = feat_ref[rows - TILE :, :]
    near_ref[3 * TILE :, :] = high_ref[...]
    for part in range(4):
        here = slice(part * TILE, (part + 1) * TILE)
        turned_ref[:, here] = jnp.transpose(near_ref[here, :])
    refs = (near_ref, turned_ref, near_rows_ref, cols_ref, edge_ref, value_ref, change_ref)
    refs += (radial_ref, narrow_ref, mix_ref, self_ref, readout_ref, message_ref, grad_ref)

    def gain_of(centre):
        kinds = lax.broadcasted_iota(jnp.int32, (TILE, table_ref.shape[0]), 1)
        picked = (cols_ref[centre, 4:5].astype(jnp.int32) == kinds).astype(jnp.float32)
        rows_of = jnp.dot(
            picked,
            table_ref[...],
            precision=lax.Precision.HIGHEST,
            preferred_element_type=jnp.float32,
        )
        return [rows_of[:, l * channels : (l + 1) * channels] for l in range(3)]

    def body(at, carry):
        base = pl.multiple_of(at * WINDOW, WINDOW)

        def results(fresh, energy, force):
            total_ref[at] = force

            if at == 0:
                new_ref[0:BLOCK, :] = fresh[BLOCK:, :]
                energy_ref[0:BLOCK] = energy[0, BLOCK:]

            if at == 1:
                new_ref[rows - BLOCK :, :] = fresh[0:BLOCK, :]
                energy_ref[rows - BLOCK :] = energy[0, 0:BLOCK]

        pair_factors(
            base, near_rows_ref, cols_ref, edge_ref.at[at], value_ref.at[at], change_ref.at[at], orders
        )
        one_tile(at, base, refs, gain_of, None, results, orders)
        return carry

    for at in range(2):
        body(at, 0)
    inner = inner_new_ref.shape[0]
    for at in range(inner):
        here = slice(BLOCK + at * TILE, BLOCK + (at + 1) * TILE)
        new_ref[here, :] = inner_new_ref[at]
        energy_ref[here] = inner_energy_ref[at, 0]
    force_ref[...] = inner_force_ref[0:3, :]
    force_ref[:, 0:TILE] += total_ref[0, 0:3, TILE:]
    force_ref[:, rows - TILE :] += total_ref[1, 0:3, 0:TILE]


def call(kernel, name, out_shape, scratch, flops, *operands, distant=()):
    whole = pl.BlockSpec(memory_space=pltpu.VMEM)
    hbm = pl.BlockSpec(memory_space=pl.ANY)
    return pl.pallas_call(
        kernel,
        out_shape=out_shape,
        in_specs=[hbm if at in distant else whole for at in range(len(operands))],
        out_specs=jax.tree.map(lambda _: whole, out_shape),
        scratch_shapes=scratch,
        compiler_params=pltpu.CompilerParams(vmem_limit_bytes=VMEM_BYTES),
        cost_estimate=pl.CostEstimate(flops=flops, bytes_accessed=4 * 2**20, transcendentals=0),
        name=name,
    )(*operands)


def from_sides(block_low, block_high):
    count = lax.axis_size(AXES)
    forward = [(i, i + 1) for i in range(count - 1)]
    backward = [(target, source) for source, target in forward]
    low = lax.ppermute(block_high, AXES, forward)
    high = lax.ppermute(block_low, AXES, backward)
    return low, high


def per_device(
    features_domain,
    arrival,
    positions,
    species,
    block_count,
    pair_block,
    radial_weights,
    species_weights,
    mix_weight,
    self_weight,
    readout,
):
    devices = lax.axis_size(AXES)
    atom_rows, feature_cols = features_domain.shape
    piece_rows = atom_rows // devices
    parcels = features_domain.reshape(devices, piece_rows, feature_cols)
    received = lax.all_to_all(parcels, AXES, split_axis=0, concat_axis=0, tiled=True)
    received = received.reshape(atom_rows, feature_cols)
    blocks = block_count.shape[0]
    bf16, f32 = jnp.bfloat16, jnp.float32
    shape = jax.ShapeDtypeStruct

    def per_slot(values):
        return jnp.broadcast_to(values[:, None], (blocks, BLOCK)).reshape(1, atom_rows)

    slot = jnp.arange(BLOCK, dtype=jnp.int32)
    live = (slot[None, :] < block_count[:, None]).reshape(1, atom_rows)
    arrival_live = jnp.where(live, arrival.reshape(1, atom_rows), -1)
    listed = (pair_block >= 0).astype(f32)
    rows = jnp.concatenate(
        [
            positions.T,
            live.astype(f32),
            species.astype(f32).reshape(1, atom_rows),
            per_slot(listed[:, 0]),
            per_slot(listed[:, 2]),
            jnp.zeros((1, atom_rows), f32),
        ],
        axis=0,
    )
    low_rows, high_rows = from_sides(rows[:, :TILE], rows[:, atom_rows - TILE :])
    species_total = species_weights.shape[0]
    one_hot = (species[:, None] == jnp.arange(species_total, dtype=jnp.int32)[None, :]).astype(f32)
    table = species_weights.reshape(species_total, -1)
    gains = jnp.dot(one_hot, table, precision=lax.Precision.HIGHEST)
    orders, _, channels = radial_weights.shape
    inner = atom_rows // TILE - 1
    subs = TILE // SUB
    stack = orders * SUB
    edges, values, changes = pl.pallas_call(
        functools.partial(pairs_kernel, orders=orders),
        grid=(inner,),
        out_shape=(
            pltpu.HBM((inner, subs, HARM, stack, WINDOW), bf16),
            pltpu.HBM((inner, subs, stack, WINDOW), bf16),
            pltpu.HBM((inner, subs, stack, WINDOW), bf16),
        ),
        in_specs=[pl.BlockSpec((8, atom_rows), lambda t: (0, 0))],
        out_specs=(
            pl.BlockSpec((1, subs, HARM, stack, WINDOW), lambda t: (t, 0, 0, 0, 0)),
            pl.BlockSpec((1, subs, stack, WINDOW), lambda t: (t, 0, 0, 0)),
            pl.BlockSpec((1, subs, stack, WINDOW), lambda t: (t, 0, 0, 0)),
        ),
        scratch_shapes=[pltpu.VMEM((atom_rows, 8), f32)],
        compiler_params=pltpu.CompilerParams(vmem_limit_bytes=VMEM_BYTES),
        cost_estimate=pl.CostEstimate(flops=10**10, bytes_accessed=40 * 2**20, transcendentals=0),
        name="pairs",
    )(rows)
    first, last = call(
        edge_tiles_kernel,
        "edge_tiles",
        (shape((TILE, feature_cols), bf16), shape((TILE, feature_cols), bf16)),
        [],
        4 * TILE * atom_rows * feature_cols,
        arrival_live,
        received,
    )
    low, high = from_sides(first, last)
    radial = radial_weights.reshape(-1, channels)
    common = (radial, mix_weight, self_weight, readout.reshape(1, -1))
    tile_flops = 4 * orders * TILE * WINDOW * channels * 25
    held = functools.partial(pltpu.with_memory_space_constraint, memory_space=pltpu.VMEM)
    distant = functools.partial(pltpu.with_memory_space_constraint, memory_space=pltpu.HBM)

    def scratch(count):
        return [
            pltpu.VMEM((PATHS, orders * SUB, channels), bf16),
            pltpu.VMEM((HARM, TILE, channels), f32),
            pltpu.VMEM((HARM, TILE, channels), bf16),
            pltpu.VMEM((count, subs, HARM, stack, WINDOW), bf16),
            pltpu.VMEM((count, subs, stack, WINDOW), bf16),
            pltpu.VMEM((count, subs, stack, WINDOW), bf16),
        ]

    feat, inner_new, inner_energy, inner_force = call(
        functools.partial(inner_kernel, orders=orders),
        "inner",
        (
            HELD((atom_rows, feature_cols), bf16),
            HELD((inner, TILE, channels), bf16),
            HELD((inner, 1, TILE), f32),
            HELD((8, atom_rows), f32),
        ),
        [pltpu.VMEM((feature_cols, atom_rows), bf16), pltpu.VMEM((atom_rows, 8), f32)]
        + scratch(inner)
        + [pltpu.SemaphoreType.DMA((inner, subs)), pltpu.SemaphoreType.DMA((inner, 2))],
        inner * tile_flops,
        arrival_live,
        received,
        first,
        last,
        rows,
        distant(edges),
        distant(values),
        distant(changes),
        gains,
        *common,
        distant=(5, 6, 7),
    )
    new_rows, energies, forces = call(
        functools.partial(outer_kernel, orders=orders),
        "outer",
        (
            shape((atom_rows, channels), bf16),
            shape((atom_rows,), f32),
            shape((3, atom_rows), f32),
        ),
        [
            pltpu.VMEM((4 * TILE, feature_cols), bf16),
            pltpu.VMEM((feature_cols, 4 * TILE), bf16),
            pltpu.VMEM((8, 4 * TILE), f32),
            pltpu.VMEM((4 * TILE, 8), f32),
        ]
        + scratch(2)
        + [pltpu.VMEM((2, 8, WINDOW), f32)],
        2 * tile_flops,
        low,
        high,
        held(feat),
        low_rows,
        rows,
        high_rows,
        table,
        *common,
        held(inner_new),
        held(inner_energy),
        held(inner_force),
    )
    return (energies, forces.T, new_rows)


def solution(mesh):
    placed = (
        P(("dom", "blk"), None),
        P(("dom", "blk")),
        P(("dom", "blk"), None),
        P(("dom", "blk")),
        P(("dom", "blk")),
        P(("dom", "blk"), None),
        P(),
        P(),
        P(),
        P(),
        P(),
    )
    return jax.shard_map(
        per_device,
        mesh=mesh,
        in_specs=placed,
        out_specs=(P(("dom", "blk")), P(("dom", "blk"), None), P(("dom", "blk"), None)),
        check_vma=False,
    )
```

```python
import functools
import math

import jax
import jax.numpy as jnp
import numpy as np
from jax import lax
from jax.experimental import pallas as pl
from jax.experimental.pallas import tpu as pltpu
from jax.sharding import PartitionSpec as P

BLOCK = 64
TILE = 2 * BLOCK
WINDOW = 4 * BLOCK
SUB = BLOCK
HARM = 9
PATHS = 7
ROOT_THREE = math.sqrt(3.0)
AXES = ("dom", "blk")
VMEM_BYTES = 40 * 1024 * 1024
HELD = pltpu.VMEM


def degree(k):
    return 0 if k == 0 else (1 if k < 4 else 2)


def polynomial(square, coefficients):
    total = jnp.full_like(square, coefficients[-1])
    for value in coefficients[-2::-1]:
        total = total * square + value
    return total


SINE = [(-1.0) ** m * math.pi ** (2 * m + 1) / math.factorial(2 * m + 1) for m in range(6)]
COSINE = [(-1.0) ** m * math.pi ** (2 * m) / math.factorial(2 * m) for m in range(7)]


def solid(x, y, z):
    return [
        None,
        x,
        y,
        z,
        ROOT_THREE * x * y,
        ROOT_THREE * y * z,
        z * z - 0.5 * (x * x + y * y),
        ROOT_THREE * z * x,
        (0.5 * ROOT_THREE) * (x * x - y * y),
    ]


def edge_tiles_kernel(chosen_ref, received_ref, first_ref, last_ref):
    rows = received_ref.shape[0]
    both = jnp.concatenate([chosen_ref[0:TILE, :], chosen_ref[rows - TILE :, :]], axis=0)
    found = jnp.dot(both, received_ref[...], preferred_element_type=jnp.float32).astype(
        jnp.bfloat16
    )
    first_ref[...] = found[0:TILE]
    last_ref[...] = found[TILE:]


def pair_factors(base, rows_ref, cols_ref, edge_at, value_at, change_at, orders):
    window = pl.ds(base, WINDOW)
    for sub in range(TILE // SUB):
        half = sub * SUB // BLOCK
        here = pl.ds(pl.multiple_of(base + (BLOCK + sub * SUB), SUB), SUB)
        column = lax.broadcasted_iota(jnp.int32, (SUB, WINDOW), 1)
        row = lax.broadcasted_iota(jnp.int32, (SUB, WINDOW), 0) + (sub * SUB + BLOCK)
        offset = column - half * BLOCK
        low = jnp.where((offset >= 0) & (offset < BLOCK), cols_ref[here, 5:6], 0.0)
        high = jnp.where(
            (offset >= 2 * BLOCK) & (offset < 3 * BLOCK), cols_ref[here, 6:7], low
        )
        same = (offset >= BLOCK) & (offset < 2 * BLOCK) & (row != column)
        keep = jnp.where(same, 1.0, high)
        x, y, z = [rows_ref[a : a + 1, window] - cols_ref[here, a : a + 1] for a in range(3)]
        spread = x * x + y * y + z * z
        room = jnp.maximum(1.0 - spread, 0.0)
        squared = room * room * keep
        envelope = squared * room
        slope = -3.0 * squared
        shifted = jnp.minimum(spread, 1.0) - 0.5
        shifted_sq = shifted * shifted
        cosine = -shifted * polynomial(shifted_sq, SINE)
        sine = polynomial(shifted_sq, COSINE)
        twice = 2.0 * cosine
        cos_prev, cos_now = jnp.ones_like(cosine), cosine
        sin_prev, sin_now = jnp.zeros_like(sine), sine
        harm = solid(x, y, z)
        for n in range(orders):
            rows = slice(n * SUB, (n + 1) * SUB)
            if n == 0:
                value, change = envelope, slope
            else:
                value = envelope * cos_now
                change = slope * cos_now - (n * math.pi) * (envelope * sin_now)
            value_at[sub, rows, :] = value.astype(jnp.bfloat16)
            change_at[sub, rows, :] = change.astype(jnp.bfloat16)
            for k in range(HARM):
                edge = value if k == 0 else value * harm[k]
                edge_at[sub, k, rows, :] = edge.astype(jnp.bfloat16)
            if n >= 1:
                cos_prev, cos_now = cos_now, twice * cos_now - cos_prev
                sin_prev, sin_now = sin_now, twice * sin_now - sin_prev


def pairs_kernel(rows_ref, edge_ref, value_ref, change_ref, cols_ref, orders):
    tile = pl.program_id(0)

    @pl.when(tile == 0)
    def _():
        cols_ref[...] = jnp.transpose(rows_ref[...])

    base = pl.multiple_of(tile * TILE, TILE)
    pair_factors(
        base, rows_ref, cols_ref, edge_ref.at[0], value_ref.at[0], change_ref.at[0], orders
    )


def spread_weights(radial_ref, narrow_ref, orders):
    for path in range(PATHS):
        for n in range(orders):
            row = radial_ref[n * PATHS + path : n * PATHS + path + 1, :]
            narrow_ref[path, n * SUB : (n + 1) * SUB, :] = jnp.broadcast_to(
                row, (SUB, row.shape[1])
            ).astype(jnp.bfloat16)


def fetch(sources, held):
    edge_hbm, value_hbm, change_hbm = sources
    edge_ref, value_ref, change_ref, edge_sem, factor_sem = held
    count, subs = edge_ref.shape[:2]

    def edges(at, sub):
        return pltpu.make_async_copy(
            edge_hbm.at[at, sub], edge_ref.at[at, sub], edge_sem.at[at, sub]
        )

    def factors(at):
        return (
            pltpu.make_async_copy(value_hbm.at[at], value_ref.at[at], factor_sem.at[at, 0]),
            pltpu.make_async_copy(change_hbm.at[at], change_ref.at[at], factor_sem.at[at, 1]),
        )

    for at in range(count):
        for sub in range(subs):
            edges(at, sub).start()
        for copy in factors(at):
            copy.start()
    return edges, factors


def one_tile(at, base, refs, gain_of, copies, results, orders, reach=(None, None)):
    feat_ref, turned_ref, rows_ref, cols_ref, edge_ref, value_ref, change_ref = refs[:7]
    radial_ref, narrow_ref, mix_ref, self_ref, readout_ref = refs[7:12]
    message_ref, grad_ref = refs[12:]
    channels = mix_ref.shape[0]
    window = pl.ds(base, WINDOW)
    centre = pl.ds(pl.multiple_of(base + BLOCK, BLOCK), TILE)
    subs = range(TILE // SUB)

    def weight(n, path):
        return radial_ref[n * PATHS + path : n * PATHS + path + 1, :]

    def piece(k):
        return feat_ref[window, k * channels : (k + 1) * channels]

    def path_sum(product, first, path):
        total = None
        for n in range(orders):
            part = product[n * SUB : (n + 1) * SUB, first : first + channels] * weight(n, path)
            total = part if total is None else total + part
        return total

    for sub in subs:
        rows = slice(sub * SUB, (sub + 1) * SUB)
        if copies is not None:
            copies[0](at, sub).wait()
        found = {}
        for k in range(0, HARM, 2):
            last = min(k + 2, HARM)
            pairs = jnp.dot(
                edge_ref[at, sub, 0],
                feat_ref[window, k * channels : last * channels],
                preferred_element_type=jnp.float32,
            )
            for which in range(k, last):
                path = 0 if which == 0 else 2 + degree(which)
                found[which] = path_sum(pairs, (which - k) * channels, path)
        for k in range(1, HARM):
            both = jnp.concatenate([piece(k), piece(0)], axis=1)
            pairs = jnp.dot(edge_ref[at, sub, k], both, preferred_element_type=jnp.float32)
            found[0] = found[0] + path_sum(pairs, 0, 4 + degree(k))
            message_ref[k, rows, :] = found[k] + path_sum(pairs, channels, degree(k))
        message_ref[0, rows, :] = found[0]

    gain = gain_of(centre)
    zero = message_ref[0]
    first = sum(message_ref[k] * message_ref[k] for k in range(1, 4))
    second = sum(message_ref[k] * message_ref[k] for k in range(4, HARM))
    basis = zero + gain[0] * (zero * zero) + gain[1] * first + gain[2] * second
    live = cols_ref[centre, 3:4]
    mixed = jnp.dot(
        basis.astype(jnp.bfloat16), mix_ref[...], preferred_element_type=jnp.float32
    ) + jnp.dot(feat_ref[centre, 0:channels], self_ref[...], preferred_element_type=jnp.float32)
    gate = 1.0 / (1.0 + jnp.exp(-mixed))
    silu = mixed * gate
    readout = readout_ref[...]
    fresh = (live * mixed).astype(jnp.bfloat16)
    energy = jnp.sum(jnp.transpose(live * (readout * silu)), axis=0, keepdims=True)
    mixed_grad = live * readout * (gate * (1.0 + mixed - silu))
    basis_grad = lax.dot_general(
        mixed_grad.astype(jnp.bfloat16),
        mix_ref[...],
        (((1,), (1,)), ((), ())),
        preferred_element_type=jnp.float32,
    )
    grad_ref[0] = (basis_grad * (1.0 + 2.0 * gain[0] * zero)).astype(jnp.bfloat16)
    for k in range(1, HARM):
        grad_ref[k] = (basis_grad * (2.0 * gain[degree(k)]) * message_ref[k]).astype(jnp.bfloat16)

    def backward(sub):
        lanes = slice(0, WINDOW) if reach[sub] is None else reach[sub]
        seen = pl.ds(pl.multiple_of(base + lanes.start, TILE), lanes.stop - lanes.start)
        rows = slice(sub * SUB, (sub + 1) * SUB)
        here = pl.ds(pl.multiple_of(base + (BLOCK + sub * SUB), SUB), SUB)
        grads = [jnp.concatenate([grad_ref[k, rows, :]] * orders, axis=0) for k in range(HARM)]
        x, y, z = [rows_ref[a : a + 1, seen] - cols_ref[here, a : a + 1] for a in range(3)]
        harm = solid(x, y, z)
        root_x, root_y, root_z = ROOT_THREE * x, ROOT_THREE * y, ROOT_THREE * z
        slopes = {
            1: {0: None},
            2: {1: None},
            3: {2: None},
            4: {0: root_y, 1: root_x},
            5: {1: root_z, 2: root_y},
            6: {0: -x, 1: -y, 2: 2.0 * z},
            7: {0: root_z, 2: root_x},
            8: {0: root_x, 1: -root_y},
        }

        def over_orders(cross, factor_ref):
            parts = [
                cross[n * SUB : (n + 1) * SUB].astype(jnp.bfloat16)
                * factor_ref[at, sub, n * SUB : (n + 1) * SUB, lanes]
                for n in range(orders)
            ]
            while len(parts) > 1:
                parts = [parts[m] + parts[m + 1] for m in range(0, len(parts), 2)]
            return parts[0].astype(jnp.float32)

        left = jnp.concatenate(
            [grads[k] * narrow_ref[0 if k == 0 else 2 + degree(k)] for k in range(HARM)], axis=1
        )
        cross = jnp.dot(left, turned_ref[:, seen], preferred_element_type=jnp.float32)
        radial_total = over_orders(cross, change_ref)
        pull = [None, None, None]
        for k in range(1, HARM):
            left = jnp.concatenate(
                [grads[0] * narrow_ref[4 + degree(k)], grads[k] * narrow_ref[degree(k)]], axis=1
            )
            both = jnp.concatenate(
                [
                    turned_ref[k * channels : (k + 1) * channels, seen],
                    turned_ref[0:channels, seen],
                ],
                axis=0,
            )
            cross = jnp.dot(left, both, preferred_element_type=jnp.float32)
            along = over_orders(cross, value_ref)
            radial_total = radial_total + over_orders(cross, change_ref) * harm[k]
            for axis, factor in slopes[k].items():
                term = along if factor is None else along * factor
                pull[axis] = term if pull[axis] is None else pull[axis] + term
        radial_total = 2.0 * radial_total
        return [pull[axis] + delta * radial_total for axis, delta in enumerate((x, y, z))]

    if copies is not None:
        for copy in copies[1](at):
            copy.wait()
    onto_window = [None, None, None]
    columns_out = [[], [], []]
    for sub in subs:
        for axis, total in enumerate(backward(sub)):
            summed = jnp.sum(total, axis=0, keepdims=True)
            if reach[sub] is not None:
                rest = jnp.zeros((1, WINDOW - summed.shape[1]), jnp.float32)
                order = [rest, summed] if reach[sub].start > 0 else [summed, rest]
                summed = jnp.concatenate(order, axis=1)
            onto_window[axis] = summed if sub == 0 else onto_window[axis] + summed
            columns_out[axis].append(jnp.sum(total, axis=1, keepdims=True))
    lane = lax.broadcasted_iota(jnp.int32, (TILE, 8), 1)
    row = lax.broadcasted_iota(jnp.int32, (8, WINDOW), 0)
    packed = jnp.zeros((TILE, 8), jnp.float32)
    pulled = jnp.zeros((8, WINDOW), jnp.float32)
    for axis in range(3):
        packed = jnp.where(lane == axis, jnp.concatenate(columns_out[axis], axis=0), packed)
        pulled = jnp.where(row == axis, onto_window[axis], pulled)
    turned = jnp.transpose(packed)
    side = jnp.zeros((8, BLOCK), jnp.float32)
    results(fresh, energy, jnp.concatenate([side, turned, side], axis=1) - pulled)


def inner_kernel(
    chosen_ref,
    received_ref,
    first_ref,
    last_ref,
    rows_ref,
    edge_hbm,
    value_hbm,
    change_hbm,
    gains_ref,
    radial_ref,
    mix_ref,
    self_ref,
    readout_ref,
    feat_ref,
    new_ref,
    energy_ref,
    force_ref,
    turned_ref,
    cols_ref,
    narrow_ref,
    message_ref,
    grad_ref,
    edge_ref,
    value_ref,
    change_ref,
    edge_sem,
    factor_sem,
    orders,
):
    held = (edge_ref, value_ref, change_ref, edge_sem, factor_sem)
    copies = fetch((edge_hbm, value_hbm, change_hbm), held)
    rows = received_ref.shape[0]
    channels = mix_ref.shape[0]
    cols_ref[...] = jnp.transpose(rows_ref[...])
    spread_weights(radial_ref, narrow_ref, orders)
    force_ref[...] = jnp.zeros_like(force_ref)
    feat_ref[0:TILE, :] = first_ref[...]
    turned_ref[:, 0:TILE] = jnp.transpose(first_ref[...])
    for part in range(1, rows // TILE - 1):
        here = slice(part * TILE, (part + 1) * TILE)
        found = jnp.dot(
            chosen_ref[here, :],
            received_ref[...],
            preferred_element_type=jnp.float32,
        ).astype(jnp.bfloat16)
        feat_ref[here, :] = found
        turned_ref[:, here] = jnp.transpose(found)
    feat_ref[rows - TILE :, :] = last_ref[...]
    turned_ref[:, rows - TILE :] = jnp.transpose(last_ref[...])
    refs = (feat_ref, turned_ref, rows_ref, cols_ref, edge_ref, value_ref, change_ref)
    refs += (radial_ref, narrow_ref, mix_ref, self_ref, readout_ref, message_ref, grad_ref)

    def gain_of(centre):
        return [gains_ref[centre, l * channels : (l + 1) * channels] for l in range(3)]

    def body(at, carry):
        base = pl.multiple_of(at * TILE, TILE)

        def results(fresh, energy, force):
            new_ref[at] = fresh
            energy_ref[at] = energy
            force_ref[:, pl.ds(base, WINDOW)] += force

        one_tile(at, base, refs, gain_of, copies, results, orders)
        return carry

    lax.fori_loop(0, edge_hbm.shape[0], body, 0)


def outer_kernel(
    low_ref,
    high_ref,
    feat_ref,
    low_rows_ref,
    rows_ref,
    high_rows_ref,
    table_ref,
    radial_ref,
    narrow_ref,
    mix_ref,
    self_ref,
    readout_ref,
    inner_new_ref,
    inner_energy_ref,
    inner_force_ref,
    new_ref,
    energy_ref,
    force_ref,
    near_ref,
    turned_ref,
    near_rows_ref,
    cols_ref,
    message_ref,
    grad_ref,
    edge_ref,
    value_ref,
    change_ref,
    total_ref,
    orders,
):
    rows = feat_ref.shape[0]
    channels = mix_ref.shape[0]
    near_rows_ref[:, 0:TILE] = low_rows_ref[...]
    near_rows_ref[:, TILE : 2 * TILE] = rows_ref[:, 0:TILE]
    near_rows_ref[:, 2 * TILE : 3 * TILE] = rows_ref[:, rows - TILE :]
    near_rows_ref[:, 3 * TILE :] = high_rows_ref[...]
    cols_ref[...] = jnp.transpose(near_rows_ref[...])
    near_ref[0:TILE, :] = low_ref[...]
    near_ref[TILE : 2 * TILE, :] = feat_ref[0:TILE, :]
    near_ref[2 * TILE : 3 * TILE, :] = feat_ref[rows - TILE :, :]
    near_ref[3 * TILE :, :] = high_ref[...]
    for part in range(4):
        here = slice(part * TILE, (part + 1) * TILE)
        turned_ref[:, here] = jnp.transpose(near_ref[here, :])
    refs = (near_ref, turned_ref, near_rows_ref, cols_ref, edge_ref, value_ref, change_ref)
    refs += (radial_ref, narrow_ref, mix_ref, self_ref, readout_ref, message_ref, grad_ref)

    def gain_of(centre):
        kinds = lax.broadcasted_iota(jnp.int32, (TILE, table_ref.shape[0]), 1)
        picked = (cols_ref[centre, 4:5].astype(jnp.int32) == kinds).astype(jnp.float32)
        rows_of = jnp.dot(
            picked,
            table_ref[...],
            precision=lax.Precision.HIGHEST,
            preferred_element_type=jnp.float32,
        )
        return [rows_of[:, l * channels : (l + 1) * channels] for l in range(3)]

    def body(at, carry):
        base = pl.multiple_of(at * WINDOW, WINDOW)

        def results(fresh, energy, force):
            total_ref[at] = force

            if at == 0:
                new_ref[0:BLOCK, :] = fresh[BLOCK:, :]
                energy_ref[0:BLOCK] = energy[0, BLOCK:]

            if at == 1:
                new_ref[rows - BLOCK :, :] = fresh[0:BLOCK, :]
                energy_ref[rows - BLOCK :] = energy[0, 0:BLOCK]

        pair_factors(
            base, near_rows_ref, cols_ref, edge_ref.at[at], value_ref.at[at], change_ref.at[at], orders
        )
        reach = (slice(TILE, WINDOW), None) if at == 0 else (None, slice(0, TILE))
        one_tile(at, base, refs, gain_of, None, results, orders, reach)
        return carry

    for at in range(2):
        body(at, 0)
    inner = inner_new_ref.shape[0]
    for at in range(inner):
        here = slice(BLOCK + at * TILE, BLOCK + (at + 1) * TILE)
        new_ref[here, :] = inner_new_ref[at]
        energy_ref[here] = inner_energy_ref[at, 0]
    force_ref[...] = inner_force_ref[0:3, :]
    force_ref[:, 0:TILE] += total_ref[0, 0:3, TILE:]
    force_ref[:, rows - TILE :] += total_ref[1, 0:3, 0:TILE]


def call(kernel, name, out_shape, scratch, flops, *operands, distant=()):
    whole = pl.BlockSpec(memory_space=pltpu.VMEM)
    hbm = pl.BlockSpec(memory_space=pl.ANY)
    return pl.pallas_call(
        kernel,
        out_shape=out_shape,
        in_specs=[hbm if at in distant else whole for at in range(len(operands))],
        out_specs=jax.tree.map(lambda _: whole, out_shape),
        scratch_shapes=scratch,
        compiler_params=pltpu.CompilerParams(vmem_limit_bytes=VMEM_BYTES),
        cost_estimate=pl.CostEstimate(flops=flops, bytes_accessed=4 * 2**20, transcendentals=0),
        name=name,
    )(*operands)


def from_sides(block_low, block_high):
    count = lax.axis_size(AXES)
    forward = [(i, i + 1) for i in range(count - 1)]
    backward = [(target, source) for source, target in forward]
    low = lax.ppermute(block_high, AXES, forward)
    high = lax.ppermute(block_low, AXES, backward)
    return low, high


def per_device(
    features_domain,
    arrival,
    positions,
    species,
    block_count,
    pair_block,
    radial_weights,
    species_weights,
    mix_weight,
    self_weight,
    readout,
):
    devices = lax.axis_size(AXES)
    atom_rows, feature_cols = features_domain.shape
    piece_rows = atom_rows // devices
    parcels = features_domain.reshape(devices, piece_rows, feature_cols)
    received = lax.all_to_all(parcels, AXES, split_axis=0, concat_axis=0, tiled=True)
    received = received.reshape(atom_rows, feature_cols)
    blocks = block_count.shape[0]
    bf16, f32 = jnp.bfloat16, jnp.float32
    shape = jax.ShapeDtypeStruct

    def per_slot(values):
        return jnp.broadcast_to(values[:, None], (blocks, BLOCK)).reshape(1, atom_rows)

    slot = jnp.arange(BLOCK, dtype=jnp.int32)
    live = (slot[None, :] < block_count[:, None]).reshape(1, atom_rows)
    arrival_live = jnp.where(live, arrival.reshape(1, atom_rows), -1).reshape(atom_rows, 1)
    chosen = (arrival_live == jnp.arange(atom_rows, dtype=jnp.int32)[None, :]).astype(bf16)
    listed = (pair_block >= 0).astype(f32)
    rows = jnp.concatenate(
        [
            positions.T,
            live.astype(f32),
            species.astype(f32).reshape(1, atom_rows),
            per_slot(listed[:, 0]),
            per_slot(listed[:, 2]),
            jnp.zeros((1, atom_rows), f32),
        ],
        axis=0,
    )
    low_rows, high_rows = from_sides(rows[:, :TILE], rows[:, atom_rows - TILE :])
    species_total = species_weights.shape[0]
    one_hot = (species[:, None] == jnp.arange(species_total, dtype=jnp.int32)[None, :]).astype(f32)
    table = species_weights.reshape(species_total, -1)
    gains = jnp.dot(one_hot, table, precision=lax.Precision.HIGHEST)
    orders, _, channels = radial_weights.shape
    inner = atom_rows // TILE - 1
    subs = TILE // SUB
    stack = orders * SUB
    edges, values, changes = pl.pallas_call(
        functools.partial(pairs_kernel, orders=orders),
        grid=(inner,),
        out_shape=(
            pltpu.HBM((inner, subs, HARM, stack, WINDOW), bf16),
            pltpu.HBM((inner, subs, stack, WINDOW), bf16),
            pltpu.HBM((inner, subs, stack, WINDOW), bf16),
        ),
        in_specs=[pl.BlockSpec((8, atom_rows), lambda t: (0, 0))],
        out_specs=(
            pl.BlockSpec((1, subs, HARM, stack, WINDOW), lambda t: (t, 0, 0, 0, 0)),
            pl.BlockSpec((1, subs, stack, WINDOW), lambda t: (t, 0, 0, 0)),
            pl.BlockSpec((1, subs, stack, WINDOW), lambda t: (t, 0, 0, 0)),
        ),
        scratch_shapes=[pltpu.VMEM((atom_rows, 8), f32)],
        compiler_params=pltpu.CompilerParams(vmem_limit_bytes=VMEM_BYTES),
        cost_estimate=pl.CostEstimate(flops=10**10, bytes_accessed=40 * 2**20, transcendentals=0),
        name="pairs",
    )(rows)
    first, last = call(
        edge_tiles_kernel,
        "edge_tiles",
        (shape((TILE, feature_cols), bf16), shape((TILE, feature_cols), bf16)),
        [],
        4 * TILE * atom_rows * feature_cols,
        chosen,
        received,
    )
    low, high = from_sides(first, last)
    radial = radial_weights.reshape(-1, channels)
    narrow = jnp.repeat(radial_weights.transpose(1, 0, 2).astype(bf16), SUB, axis=1)
    common = (radial, mix_weight, self_weight, readout.reshape(1, -1))
    tile_flops = 4 * orders * TILE * WINDOW * channels * 25
    held = functools.partial(pltpu.with_memory_space_constraint, memory_space=pltpu.VMEM)
    distant = functools.partial(pltpu.with_memory_space_constraint, memory_space=pltpu.HBM)

    def scratch(count):
        return [
            pltpu.VMEM((HARM, TILE, channels), f32),
            pltpu.VMEM((HARM, TILE, channels), bf16),
            pltpu.VMEM((count, subs, HARM, stack, WINDOW), bf16),
            pltpu.VMEM((count, subs, stack, WINDOW), bf16),
            pltpu.VMEM((count, subs, stack, WINDOW), bf16),
        ]

    feat, inner_new, inner_energy, inner_force = call(
        functools.partial(inner_kernel, orders=orders),
        "inner",
        (
            HELD((atom_rows, feature_cols), bf16),
            HELD((inner, TILE, channels), bf16),
            HELD((inner, 1, TILE), f32),
            HELD((8, atom_rows), f32),
        ),
        [
            pltpu.VMEM((feature_cols, atom_rows), bf16),
            pltpu.VMEM((atom_rows, 8), f32),
            pltpu.VMEM((PATHS, orders * SUB, channels), bf16),
        ]
        + scratch(inner)
        + [pltpu.SemaphoreType.DMA((inner, subs)), pltpu.SemaphoreType.DMA((inner, 2))],
        inner * tile_flops,
        chosen,
        received,
        first,
        last,
        rows,
        distant(edges),
        distant(values),
        distant(changes),
        gains,
        *common,
        distant=(5, 6, 7),
    )
    new_rows, energies, forces = call(
        functools.partial(outer_kernel, orders=orders),
        "outer",
        (
            shape((atom_rows, channels), bf16),
            shape((atom_rows,), f32),
            shape((3, atom_rows), f32),
        ),
        [
            pltpu.VMEM((4 * TILE, feature_cols), bf16),
            pltpu.VMEM((feature_cols, 4 * TILE), bf16),
            pltpu.VMEM((8, 4 * TILE), f32),
            pltpu.VMEM((4 * TILE, 8), f32),
        ]
        + scratch(2)
        + [pltpu.VMEM((2, 8, WINDOW), f32)],
        2 * tile_flops,
        low,
        high,
        held(feat),
        low_rows,
        rows,
        high_rows,
        table,
        radial,
        narrow,
        *common[1:],
        held(inner_new),
        held(inner_energy),
        held(inner_force),
    )
    return (energies, forces.T, new_rows)


def solution(mesh):
    placed = (
        P(("dom", "blk"), None),
        P(("dom", "blk")),
        P(("dom", "blk"), None),
        P(("dom", "blk")),
        P(("dom", "blk")),
        P(("dom", "blk"), None),
        P(),
        P(),
        P(),
        P(),
        P(),
    )
    return jax.shard_map(
        per_device,
        mesh=mesh,
        in_specs=placed,
        out_specs=(P(("dom", "blk")), P(("dom", "blk"), None), P(("dom", "blk"), None)),
        check_vma=False,
    )
```

```python
import functools
import math

import jax
import jax.numpy as jnp
import numpy as np
from jax import lax
from jax.experimental import pallas as pl
from jax.experimental.pallas import tpu as pltpu
from jax.sharding import PartitionSpec as P

BLOCK = 64
TILE = 2 * BLOCK
WINDOW = 4 * BLOCK
SUB = BLOCK
HARM = 9
PATHS = 7
ROOT_THREE = math.sqrt(3.0)
AXES = ("dom", "blk")
VMEM_BYTES = 36 * 1024 * 1024
HELD = pltpu.VMEM


def degree(k):
    return 0 if k == 0 else (1 if k < 4 else 2)


def polynomial(square, coefficients):
    total = jnp.full_like(square, coefficients[-1])
    for value in coefficients[-2::-1]:
        total = total * square + value
    return total


SINE = [(-1.0) ** m * math.pi ** (2 * m + 1) / math.factorial(2 * m + 1) for m in range(6)]
COSINE = [(-1.0) ** m * math.pi ** (2 * m) / math.factorial(2 * m) for m in range(7)]


def solid(x, y, z):
    return [
        None,
        x,
        y,
        z,
        ROOT_THREE * x * y,
        ROOT_THREE * y * z,
        z * z - 0.5 * (x * x + y * y),
        ROOT_THREE * z * x,
        (0.5 * ROOT_THREE) * (x * x - y * y),
    ]


def edge_tiles_kernel(chosen_ref, received_ref, first_ref, last_ref):
    rows = received_ref.shape[0]
    both = jnp.concatenate([chosen_ref[0:TILE, :], chosen_ref[rows - TILE :, :]], axis=0)
    found = jnp.dot(both, received_ref[...], preferred_element_type=jnp.float32).astype(
        jnp.bfloat16
    )
    first_ref[...] = found[0:TILE]
    last_ref[...] = found[TILE:]


def pair_factors(base, rows_ref, cols_ref, edge_at, value_at, change_at, orders):
    window = pl.ds(base, WINDOW)
    for sub in range(TILE // SUB):
        half = sub * SUB // BLOCK
        here = pl.ds(pl.multiple_of(base + (BLOCK + sub * SUB), SUB), SUB)
        column = lax.broadcasted_iota(jnp.int32, (SUB, WINDOW), 1)
        row = lax.broadcasted_iota(jnp.int32, (SUB, WINDOW), 0) + (sub * SUB + BLOCK)
        offset = column - half * BLOCK
        low = jnp.where((offset >= 0) & (offset < BLOCK), cols_ref[here, 5:6], 0.0)
        high = jnp.where(
            (offset >= 2 * BLOCK) & (offset < 3 * BLOCK), cols_ref[here, 6:7], low
        )
        same = (offset >= BLOCK) & (offset < 2 * BLOCK) & (row != column)
        keep = jnp.where(same, 1.0, high)
        x, y, z = [rows_ref[a : a + 1, window] - cols_ref[here, a : a + 1] for a in range(3)]
        spread = x * x + y * y + z * z
        room = jnp.maximum(1.0 - spread, 0.0)
        squared = room * room * keep
        envelope = squared * room
        slope = -3.0 * squared
        shifted = jnp.minimum(spread, 1.0) - 0.5
        shifted_sq = shifted * shifted
        cosine = -shifted * polynomial(shifted_sq, SINE)
        sine = polynomial(shifted_sq, COSINE)
        twice = 2.0 * cosine
        cos_prev, cos_now = jnp.ones_like(cosine), cosine
        sin_prev, sin_now = jnp.zeros_like(sine), sine
        harm = solid(x, y, z)
        for n in range(orders):
            rows = slice(n * SUB, (n + 1) * SUB)
            if n == 0:
                value, change = envelope, slope
            else:
                value = envelope * cos_now
                change = slope * cos_now - (n * math.pi) * (envelope * sin_now)
            value_at[sub, rows, :] = value.astype(jnp.bfloat16)
            change_at[sub, rows, :] = change.astype(jnp.bfloat16)
            for k in range(HARM):
                edge = value if k == 0 else value * harm[k]
                edge_at[sub, k, rows, :] = edge.astype(jnp.bfloat16)
            if n >= 1:
                cos_prev, cos_now = cos_now, twice * cos_now - cos_prev
                sin_prev, sin_now = sin_now, twice * sin_now - sin_prev


def pairs_kernel(rows_ref, edge_ref, value_ref, change_ref, cols_ref, orders):
    tile = pl.program_id(0)

    @pl.when(tile == 0)
    def _():
        cols_ref[...] = jnp.transpose(rows_ref[...])

    base = pl.multiple_of(tile * TILE, TILE)
    pair_factors(
        base, rows_ref, cols_ref, edge_ref.at[0], value_ref.at[0], change_ref.at[0], orders
    )


def spread_weights(radial_ref, narrow_ref, orders):
    for path in range(PATHS):
        for n in range(orders):
            row = radial_ref[n * PATHS + path : n * PATHS + path + 1, :]
            narrow_ref[path, n * SUB : (n + 1) * SUB, :] = jnp.broadcast_to(
                row, (SUB, row.shape[1])
            ).astype(jnp.bfloat16)


def fetch(sources, held):
    edge_hbm, value_hbm, change_hbm = sources
    edge_ref, value_ref, change_ref, edge_sem, factor_sem = held
    count, subs = edge_ref.shape[:2]

    def edges(at, sub):
        return pltpu.make_async_copy(
            edge_hbm.at[at, sub], edge_ref.at[at, sub], edge_sem.at[at, sub]
        )

    def factors(at):
        return (
            pltpu.make_async_copy(value_hbm.at[at], value_ref.at[at], factor_sem.at[at, 0]),
            pltpu.make_async_copy(change_hbm.at[at], change_ref.at[at], factor_sem.at[at, 1]),
        )

    for at in range(count):
        for sub in range(subs):
            edges(at, sub).start()
        for copy in factors(at):
            copy.start()
    return edges, factors


def one_tile(at, base, refs, gain_of, copies, results, orders, reach=(None, None)):
    feat_ref, turned_ref, rows_ref, cols_ref, edge_ref, value_ref, change_ref = refs[:7]
    radial_ref, narrow_ref, mix_ref, self_ref, readout_ref = refs[7:12]
    message_ref, grad_ref = refs[12:]
    channels = mix_ref.shape[0]
    window = pl.ds(base, WINDOW)
    centre = pl.ds(pl.multiple_of(base + BLOCK, BLOCK), TILE)
    subs = range(TILE // SUB)

    def weight(n, path):
        return radial_ref[n * PATHS + path : n * PATHS + path + 1, :]

    def piece(k):
        return feat_ref[window, k * channels : (k + 1) * channels]

    def path_sum(product, first, path):
        total = None
        for n in range(orders):
            part = product[n * SUB : (n + 1) * SUB, first : first + channels] * weight(n, path)
            total = part if total is None else total + part
        return total

    for sub in subs:
        rows = slice(sub * SUB, (sub + 1) * SUB)
        if copies is not None:
            copies[0](at, sub).wait()
        found = {}
        for k in range(0, HARM, 2):
            last = min(k + 2, HARM)
            pairs = jnp.dot(
                edge_ref[at, sub, 0],
                feat_ref[window, k * channels : last * channels],
                preferred_element_type=jnp.float32,
            )
            for which in range(k, last):
                path = 0 if which == 0 else 2 + degree(which)
                found[which] = path_sum(pairs, (which - k) * channels, path)
        for k in range(1, HARM):
            both = jnp.concatenate([piece(k), piece(0)], axis=1)
            pairs = jnp.dot(edge_ref[at, sub, k], both, preferred_element_type=jnp.float32)
            found[0] = found[0] + path_sum(pairs, 0, 4 + degree(k))
            message_ref[k, rows, :] = found[k] + path_sum(pairs, channels, degree(k))
        message_ref[0, rows, :] = found[0]

    gain = gain_of(centre)
    zero = message_ref[0]
    first = sum(message_ref[k] * message_ref[k] for k in range(1, 4))
    second = sum(message_ref[k] * message_ref[k] for k in range(4, HARM))
    basis = zero + gain[0] * (zero * zero) + gain[1] * first + gain[2] * second
    live = cols_ref[centre, 3:4]
    mixed = jnp.dot(
        basis.astype(jnp.bfloat16), mix_ref[...], preferred_element_type=jnp.float32
    ) + jnp.dot(feat_ref[centre, 0:channels], self_ref[...], preferred_element_type=jnp.float32)
    gate = 1.0 / (1.0 + jnp.exp(-mixed))
    silu = mixed * gate
    readout = readout_ref[...]
    fresh = (live * mixed).astype(jnp.bfloat16)
    energy = jnp.sum(jnp.transpose(live * (readout * silu)), axis=0, keepdims=True)
    mixed_grad = live * readout * (gate * (1.0 + mixed - silu))
    basis_grad = lax.dot_general(
        mixed_grad.astype(jnp.bfloat16),
        mix_ref[...],
        (((1,), (1,)), ((), ())),
        preferred_element_type=jnp.float32,
    )
    grad_ref[0] = (basis_grad * (1.0 + 2.0 * gain[0] * zero)).astype(jnp.bfloat16)
    for k in range(1, HARM):
        grad_ref[k] = (basis_grad * (2.0 * gain[degree(k)]) * message_ref[k]).astype(jnp.bfloat16)

    def backward(sub):
        lanes = slice(0, WINDOW) if reach[sub] is None else reach[sub]
        seen = pl.ds(pl.multiple_of(base + lanes.start, TILE), lanes.stop - lanes.start)
        rows = slice(sub * SUB, (sub + 1) * SUB)
        here = pl.ds(pl.multiple_of(base + (BLOCK + sub * SUB), SUB), SUB)
        grads = [jnp.concatenate([grad_ref[k, rows, :]] * orders, axis=0) for k in range(HARM)]
        x, y, z = [rows_ref[a : a + 1, seen] - cols_ref[here, a : a + 1] for a in range(3)]
        harm = solid(x, y, z)
        root_x, root_y, root_z = ROOT_THREE * x, ROOT_THREE * y, ROOT_THREE * z
        slopes = {
            1: {0: None},
            2: {1: None},
            3: {2: None},
            4: {0: root_y, 1: root_x},
            5: {1: root_z, 2: root_y},
            6: {0: -x, 1: -y, 2: 2.0 * z},
            7: {0: root_z, 2: root_x},
            8: {0: root_x, 1: -root_y},
        }

        def over_orders(cross, factor_ref):
            parts = [
                cross[n * SUB : (n + 1) * SUB].astype(jnp.bfloat16)
                * factor_ref[at, sub, n * SUB : (n + 1) * SUB, lanes]
                for n in range(orders)
            ]
            while len(parts) > 1:
                parts = [parts[m] + parts[m + 1] for m in range(0, len(parts), 2)]
            return parts[0].astype(jnp.float32)

        left = jnp.concatenate(
            [grads[k] * narrow_ref[0 if k == 0 else 2 + degree(k)] for k in range(HARM)], axis=1
        )
        cross = jnp.dot(left, turned_ref[:, seen], preferred_element_type=jnp.float32)
        radial_total = over_orders(cross, change_ref)
        pull = [None, None, None]
        for k in range(1, HARM):
            left = jnp.concatenate(
                [grads[0] * narrow_ref[4 + degree(k)], grads[k] * narrow_ref[degree(k)]], axis=1
            )
            both = jnp.concatenate(
                [
                    turned_ref[k * channels : (k + 1) * channels, seen],
                    turned_ref[0:channels, seen],
                ],
                axis=0,
            )
            cross = jnp.dot(left, both, preferred_element_type=jnp.float32)
            along = over_orders(cross, value_ref)
            radial_total = radial_total + over_orders(cross, change_ref) * harm[k]
            for axis, factor in slopes[k].items():
                term = along if factor is None else along * factor
                pull[axis] = term if pull[axis] is None else pull[axis] + term
        radial_total = 2.0 * radial_total
        return [pull[axis] + delta * radial_total for axis, delta in enumerate((x, y, z))]

    if copies is not None:
        for copy in copies[1](at):
            copy.wait()
    onto_window = [None, None, None]
    columns_out = [[], [], []]
    for sub in subs:
        for axis, total in enumerate(backward(sub)):
            summed = jnp.sum(total, axis=0, keepdims=True)
            if reach[sub] is not None:
                rest = jnp.zeros((1, WINDOW - summed.shape[1]), jnp.float32)
                order = [rest, summed] if reach[sub].start > 0 else [summed, rest]
                summed = jnp.concatenate(order, axis=1)
            onto_window[axis] = summed if sub == 0 else onto_window[axis] + summed
            columns_out[axis].append(jnp.sum(total, axis=1, keepdims=True))
    lane = lax.broadcasted_iota(jnp.int32, (TILE, 8), 1)
    row = lax.broadcasted_iota(jnp.int32, (8, WINDOW), 0)
    packed = jnp.zeros((TILE, 8), jnp.float32)
    pulled = jnp.zeros((8, WINDOW), jnp.float32)
    for axis in range(3):
        packed = jnp.where(lane == axis, jnp.concatenate(columns_out[axis], axis=0), packed)
        pulled = jnp.where(row == axis, onto_window[axis], pulled)
    turned = jnp.transpose(packed)
    side = jnp.zeros((8, BLOCK), jnp.float32)
    results(fresh, energy, jnp.concatenate([side, turned, side], axis=1) - pulled)


def inner_kernel(
    chosen_ref,
    received_ref,
    first_ref,
    last_ref,
    rows_ref,
    edge_hbm,
    value_hbm,
    change_hbm,
    gains_ref,
    radial_ref,
    mix_ref,
    self_ref,
    readout_ref,
    feat_ref,
    new_ref,
    energy_ref,
    force_ref,
    turned_ref,
    cols_ref,
    narrow_ref,
    message_ref,
    grad_ref,
    edge_ref,
    value_ref,
    change_ref,
    edge_sem,
    factor_sem,
    orders,
):
    held = (edge_ref, value_ref, change_ref, edge_sem, factor_sem)
    copies = fetch((edge_hbm, value_hbm, change_hbm), held)
    rows = received_ref.shape[0]
    channels = mix_ref.shape[0]
    cols_ref[...] = jnp.transpose(rows_ref[...])
    spread_weights(radial_ref, narrow_ref, orders)
    force_ref[...] = jnp.zeros_like(force_ref)
    feat_ref[0:TILE, :] = first_ref[...]
    turned_ref[:, 0:TILE] = jnp.transpose(first_ref[...])
    for part in range(1, rows // TILE - 1):
        here = slice(part * TILE, (part + 1) * TILE)
        found = jnp.dot(
            chosen_ref[here, :],
            received_ref[...],
            preferred_element_type=jnp.float32,
        ).astype(jnp.bfloat16)
        feat_ref[here, :] = found
        turned_ref[:, here] = jnp.transpose(found)
    feat_ref[rows - TILE :, :] = last_ref[...]
    turned_ref[:, rows - TILE :] = jnp.transpose(last_ref[...])
    refs = (feat_ref, turned_ref, rows_ref, cols_ref, edge_ref, value_ref, change_ref)
    refs += (radial_ref, narrow_ref, mix_ref, self_ref, readout_ref, message_ref, grad_ref)

    def gain_of(centre):
        return [gains_ref[centre, l * channels : (l + 1) * channels] for l in range(3)]

    def body(at, carry):
        base = pl.multiple_of(at * TILE, TILE)

        def results(fresh, energy, force):
            new_ref[at] = fresh
            energy_ref[at] = energy
            force_ref[:, pl.ds(base, WINDOW)] += force

        one_tile(at, base, refs, gain_of, copies, results, orders)
        return carry

    lax.fori_loop(0, edge_hbm.shape[0], body, 0)


def outer_kernel(
    low_ref,
    high_ref,
    feat_ref,
    low_rows_ref,
    rows_ref,
    high_rows_ref,
    table_ref,
    radial_ref,
    narrow_ref,
    mix_ref,
    self_ref,
    readout_ref,
    inner_new_ref,
    inner_energy_ref,
    inner_force_ref,
    new_ref,
    energy_ref,
    force_ref,
    near_ref,
    turned_ref,
    near_rows_ref,
    cols_ref,
    message_ref,
    grad_ref,
    edge_ref,
    value_ref,
    change_ref,
    total_ref,
    orders,
):
    rows = feat_ref.shape[0]
    channels = mix_ref.shape[0]
    near_rows_ref[:, 0:TILE] = low_rows_ref[...]
    near_rows_ref[:, TILE : 2 * TILE] = rows_ref[:, 0:TILE]
    near_rows_ref[:, 2 * TILE : 3 * TILE] = rows_ref[:, rows - TILE :]
    near_rows_ref[:, 3 * TILE :] = high_rows_ref[...]
    cols_ref[...] = jnp.transpose(near_rows_ref[...])
    near_ref[0:TILE, :] = low_ref[...]
    near_ref[TILE : 2 * TILE, :] = feat_ref[0:TILE, :]
    near_ref[2 * TILE : 3 * TILE, :] = feat_ref[rows - TILE :, :]
    near_ref[3 * TILE :, :] = high_ref[...]
    for part in range(4):
        here = slice(part * TILE, (part + 1) * TILE)
        turned_ref[:, here] = jnp.transpose(near_ref[here, :])
    refs = (near_ref, turned_ref, near_rows_ref, cols_ref, edge_ref, value_ref, change_ref)
    refs += (radial_ref, narrow_ref, mix_ref, self_ref, readout_ref, message_ref, grad_ref)

    def gain_of(centre):
        kinds = lax.broadcasted_iota(jnp.int32, (TILE, table_ref.shape[0]), 1)
        picked = (cols_ref[centre, 4:5].astype(jnp.int32) == kinds).astype(jnp.float32)
        rows_of = jnp.dot(
            picked,
            table_ref[...],
            precision=lax.Precision.HIGHEST,
            preferred_element_type=jnp.float32,
        )
        return [rows_of[:, l * channels : (l + 1) * channels] for l in range(3)]

    def body(at, carry):
        base = pl.multiple_of(at * WINDOW, WINDOW)

        def results(fresh, energy, force):
            total_ref[at] = force

            if at == 0:
                new_ref[0:BLOCK, :] = fresh[BLOCK:, :]
                energy_ref[0:BLOCK] = energy[0, BLOCK:]

            if at == 1:
                new_ref[rows - BLOCK :, :] = fresh[0:BLOCK, :]
                energy_ref[rows - BLOCK :] = energy[0, 0:BLOCK]

        pair_factors(
            base, near_rows_ref, cols_ref, edge_ref.at[at], value_ref.at[at], change_ref.at[at], orders
        )
        reach = (slice(TILE, WINDOW), None) if at == 0 else (None, slice(0, TILE))
        one_tile(at, base, refs, gain_of, None, results, orders, reach)
        return carry

    for at in range(2):
        body(at, 0)
    inner = inner_new_ref.shape[0]
    for at in range(inner):
        here = slice(BLOCK + at * TILE, BLOCK + (at + 1) * TILE)
        new_ref[here, :] = inner_new_ref[at]
        energy_ref[here] = inner_energy_ref[at, 0]
    force_ref[...] = inner_force_ref[0:3, :]
    force_ref[:, 0:TILE] += total_ref[0, 0:3, TILE:]
    force_ref[:, rows - TILE :] += total_ref[1, 0:3, 0:TILE]


def call(kernel, name, out_shape, scratch, flops, *operands, distant=()):
    whole = pl.BlockSpec(memory_space=pltpu.VMEM)
    hbm = pl.BlockSpec(memory_space=pl.ANY)
    return pl.pallas_call(
        kernel,
        out_shape=out_shape,
        in_specs=[hbm if at in distant else whole for at in range(len(operands))],
        out_specs=jax.tree.map(lambda _: whole, out_shape),
        scratch_shapes=scratch,
        compiler_params=pltpu.CompilerParams(vmem_limit_bytes=VMEM_BYTES),
        cost_estimate=pl.CostEstimate(flops=flops, bytes_accessed=4 * 2**20, transcendentals=0),
        name=name,
    )(*operands)


def from_sides(block_low, block_high):
    count = lax.axis_size(AXES)
    forward = [(i, i + 1) for i in range(count - 1)]
    backward = [(target, source) for source, target in forward]
    low = lax.ppermute(block_high, AXES, forward)
    high = lax.ppermute(block_low, AXES, backward)
    return low, high


def per_device(
    features_domain,
    arrival,
    positions,
    species,
    block_count,
    pair_block,
    radial_weights,
    species_weights,
    mix_weight,
    self_weight,
    readout,
):
    devices = lax.axis_size(AXES)
    atom_rows, feature_cols = features_domain.shape
    piece_rows = atom_rows // devices
    parcels = features_domain.reshape(devices, piece_rows, feature_cols)
    received = lax.all_to_all(parcels, AXES, split_axis=0, concat_axis=0, tiled=True)
    received = received.reshape(atom_rows, feature_cols)
    blocks = block_count.shape[0]
    bf16, f32 = jnp.bfloat16, jnp.float32
    shape = jax.ShapeDtypeStruct

    def per_slot(values):
        return jnp.broadcast_to(values[:, None], (blocks, BLOCK)).reshape(1, atom_rows)

    slot = jnp.arange(BLOCK, dtype=jnp.int32)
    live = (slot[None, :] < block_count[:, None]).reshape(1, atom_rows)
    arrival_live = jnp.where(live, arrival.reshape(1, atom_rows), -1).reshape(atom_rows, 1)
    chosen = (arrival_live == jnp.arange(atom_rows, dtype=jnp.int32)[None, :]).astype(bf16)
    listed = (pair_block >= 0).astype(f32)
    rows = jnp.concatenate(
        [
            positions.T,
            live.astype(f32),
            species.astype(f32).reshape(1, atom_rows),
            per_slot(listed[:, 0]),
            per_slot(listed[:, 2]),
            jnp.zeros((1, atom_rows), f32),
        ],
        axis=0,
    )
    low_rows, high_rows = from_sides(rows[:, :TILE], rows[:, atom_rows - TILE :])
    species_total = species_weights.shape[0]
    one_hot = (species[:, None] == jnp.arange(species_total, dtype=jnp.int32)[None, :]).astype(f32)
    table = species_weights.reshape(species_total, -1)
    gains = jnp.dot(one_hot, table, precision=lax.Precision.HIGHEST)
    orders, _, channels = radial_weights.shape
    inner = atom_rows // TILE - 1
    subs = TILE // SUB
    stack = orders * SUB
    edges, values, changes = pl.pallas_call(
        functools.partial(pairs_kernel, orders=orders),
        grid=(inner,),
        out_shape=(
            pltpu.HBM((inner, subs, HARM, stack, WINDOW), bf16),
            pltpu.HBM((inner, subs, stack, WINDOW), bf16),
            pltpu.HBM((inner, subs, stack, WINDOW), bf16),
        ),
        in_specs=[pl.BlockSpec((8, atom_rows), lambda t: (0, 0))],
        out_specs=(
            pl.BlockSpec((1, subs, HARM, stack, WINDOW), lambda t: (t, 0, 0, 0, 0)),
            pl.BlockSpec((1, subs, stack, WINDOW), lambda t: (t, 0, 0, 0)),
            pl.BlockSpec((1, subs, stack, WINDOW), lambda t: (t, 0, 0, 0)),
        ),
        scratch_shapes=[pltpu.VMEM((atom_rows, 8), f32)],
        compiler_params=pltpu.CompilerParams(vmem_limit_bytes=VMEM_BYTES),
        cost_estimate=pl.CostEstimate(flops=10**10, bytes_accessed=40 * 2**20, transcendentals=0),
        name="pairs",
    )(rows)
    first, last = call(
        edge_tiles_kernel,
        "edge_tiles",
        (shape((TILE, feature_cols), bf16), shape((TILE, feature_cols), bf16)),
        [],
        4 * TILE * atom_rows * feature_cols,
        chosen,
        received,
    )
    low, high = from_sides(first, last)
    radial = radial_weights.reshape(-1, channels)
    narrow = jnp.repeat(radial_weights.transpose(1, 0, 2).astype(bf16), SUB, axis=1)
    common = (radial, mix_weight, self_weight, readout.reshape(1, -1))
    tile_flops = 4 * orders * TILE * WINDOW * channels * 25
    held = functools.partial(pltpu.with_memory_space_constraint, memory_space=pltpu.VMEM)
    distant = functools.partial(pltpu.with_memory_space_constraint, memory_space=pltpu.HBM)

    def scratch(count):
        return [
            pltpu.VMEM((HARM, TILE, channels), f32),
            pltpu.VMEM((HARM, TILE, channels), bf16),
            pltpu.VMEM((count, subs, HARM, stack, WINDOW), bf16),
            pltpu.VMEM((count, subs, stack, WINDOW), bf16),
            pltpu.VMEM((count, subs, stack, WINDOW), bf16),
        ]

    feat, inner_new, inner_energy, inner_force = call(
        functools.partial(inner_kernel, orders=orders),
        "inner",
        (
            HELD((atom_rows, feature_cols), bf16),
            HELD((inner, TILE, channels), bf16),
            HELD((inner, 1, TILE), f32),
            HELD((8, atom_rows), f32),
        ),
        [
            pltpu.VMEM((feature_cols, atom_rows), bf16),
            pltpu.VMEM((atom_rows, 8), f32),
            pltpu.VMEM((PATHS, orders * SUB, channels), bf16),
        ]
        + scratch(inner)
        + [pltpu.SemaphoreType.DMA((inner, subs)), pltpu.SemaphoreType.DMA((inner, 2))],
        inner * tile_flops,
        chosen,
        received,
        first,
        last,
        rows,
        distant(edges),
        distant(values),
        distant(changes),
        gains,
        *common,
        distant=(5, 6, 7),
    )
    new_rows, energies, forces = call(
        functools.partial(outer_kernel, orders=orders),
        "outer",
        (
            shape((atom_rows, channels), bf16),
            shape((atom_rows,), f32),
            shape((3, atom_rows), f32),
        ),
        [
            pltpu.VMEM((4 * TILE, feature_cols), bf16),
            pltpu.VMEM((feature_cols, 4 * TILE), bf16),
            pltpu.VMEM((8, 4 * TILE), f32),
            pltpu.VMEM((4 * TILE, 8), f32),
        ]
        + scratch(2)
        + [pltpu.VMEM((2, 8, WINDOW), f32)],
        2 * tile_flops,
        low,
        high,
        held(feat),
        low_rows,
        rows,
        high_rows,
        table,
        radial,
        narrow,
        *common[1:],
        held(inner_new),
        held(inner_energy),
        held(inner_force),
    )
    return (energies, forces.T, new_rows)


def solution(mesh):
    placed = (
        P(("dom", "blk"), None),
        P(("dom", "blk")),
        P(("dom", "blk"), None),
        P(("dom", "blk")),
        P(("dom", "blk")),
        P(("dom", "blk"), None),
        P(),
        P(),
        P(),
        P(),
        P(),
    )
    return jax.shard_map(
        per_device,
        mesh=mesh,
        in_specs=placed,
        out_specs=(P(("dom", "blk")), P(("dom", "blk"), None), P(("dom", "blk"), None)),
        check_vma=False,
    )
```
